32 devices in a mesh: wide: 8 (over z, y), narrow: 4 (over x, core).
Axes of the slice: x: 2, y: 2, z: 4, core: 2. Of those that a mesh axis runs over, the one named last changes fastest.
Arguments:
- state: bfloat16 [1024, 1024, 128], P(('wide', 'narrow')), may hold values from -6 to 6
- group_of: int32 [1024], replicated, may hold values from 0 to 1023, as said below
- w_in: bfloat16 [1024, 1024], replicated, may hold values from -0.1875 to 0.1875
- w_out: bfloat16 [1024, 1024], replicated, may hold values from -0.1875 to 0.1875
- w_flux: bfloat16 [32, 1024], replicated, may hold values from -0.1875 to 0.1875
- owner: int32 [131072, 1], P(('wide', 'narrow')), may hold values from 0 to 31; in each aligned block of 4096 rows (0 to 4095, 4096 to 8191, ...) at most 256 rows name the same one
- ocean_slot: int32 [131072], P(('wide', 'narrow')), may hold values from 0 to 511
- remap_weight: float32 [131072], P(('wide', 'narrow')), may hold values from 0.25 to 4
Outputs:
- new_state: bfloat16 [1024, 1024, 128], P(('wide', 'narrow'))
- ocean: float32 [32, 16384], P(None, ('wide', 'narrow'))
The draws below stay inside these ranges and needn't reach their ends.
Inputs may be any that keep to these rules, and one draw needn't show every extreme that they name: group_of is a permutation of the blocks. Block p = ((w * 4 + n) * 32 + s) keeps n and s; for each n exactly 4 slots s move, each to wide index (w + c) modulo the wide size with a nonzero c of its own, and all other blocks stay.
All inputs are finite; a program needn't handle non-finite values.
Results may differ from the reference program's by a relative error of at most 0.0044.
Values may be sent and summed in bfloat16 or wider, within the bound.
No kernel may reach another device: no remote copies, remote signals or barrier semaphores. Data moves between devices by JAX's collectives and lax.ppermute only.
A program may use at most 192 MiB of HBM per device.

```python
import math
import jax
import jax.numpy as jnp
import numpy as np
from jax import lax

LEV = 128
VARS = 8
HID = 1024
NFLUX = 32
COLS = 128
BLK_DEV = 32
OCN_DEV = 512
MOVE = 4
NBLK = 1024
OCEANS = 16384
CAP = 256
N_WIDE = 8
N_NARROW = 4
DEVICES = 32


def draw_group_of(key, part):
    keys = jax.random.split(jax.random.fold_in(key, 11), N_NARROW)

    def band_shifts(band_key):
        first, second = jax.random.split(band_key)
        order = jax.random.permutation(first, BLK_DEV)
        shifts = jax.random.permutation(second, N_WIDE - 1)[:MOVE].astype(jnp.int32) + 1
        return jnp.zeros((BLK_DEV,), jnp.int32).at[order[:MOVE]].set(shifts)
    shift_table = jax.vmap(band_shifts)(keys)
    wide_idx = jnp.arange(N_WIDE, dtype=jnp.int32)[:, None, None]
    band_idx = jnp.arange(N_NARROW, dtype=jnp.int32)[None, :, None]
    slot_idx = jnp.arange(BLK_DEV, dtype=jnp.int32)[None, None, :]
    target_wide = (wide_idx + shift_table[None, :, :]) % N_WIDE
    dest = (target_wide * N_NARROW + band_idx) * BLK_DEV + slot_idx
    return dest.reshape(-1).astype(jnp.int32)


def place_ends(entries, rng, least, largest):
    extent = entries.shape
    spot = [jax.random.randint(jax.random.fold_in(rng, axis), (), 0, extent[axis]) for axis in range(len(extent))]
    entries = entries.at[tuple(spot)].set(least)
    longest = extent.index(max(extent))
    spot[longest] = (spot[longest] + 1) % extent[longest]
    return entries.at[tuple(spot)].set(largest)


def level_of(own_key, extent, shards, least, high):
    gain = 1.0
    for dim, shards_of in shards:
        heights = jax.random.uniform(jax.random.fold_in(jax.random.fold_in(own_key, 6), dim), (shards_of,), jnp.float32, least / len(shards), high / len(shards))
        gain = gain * jnp.repeat(jnp.exp(heights), extent[dim] // shards_of).reshape((-1,) + (1,) * (len(extent) - 1 - dim))
    return gain


def shared_out(own_key, own, number, rows, amount, top, limit, skew):
    ranking = jax.random.permutation(own_key, amount)
    crowded, common = shares(amount, rows * top, limit, skew, True), shares(amount, rows * top, limit, skew, False)
    places = jnp.arange(amount)

    def named(tallies, rotation):
        used = int((tallies > 0).sum())
        fixed = max(1, used // 4)
        shifted = fixed + (places - fixed + rotation * (used - fixed)) % max(1, amount - fixed)
        return jnp.zeros((amount,), jnp.int32).at[ranking[jnp.where(places < fixed, places, shifted)]].set(jnp.asarray(tallies, jnp.int32))

    tallies = jnp.where(number % 4 == 0, named(crowded, number // 4), named(common, number - number // 4 - 1))
    mixed = jax.random.permutation(jax.random.fold_in(own, 3), amount)
    donor, receiver = mixed[0:amount // 2 * 2:2], mixed[1:amount // 2 * 2:2]
    room = jnp.minimum(tallies[donor] - 1, limit - tallies[receiver]) // 2
    room = jnp.where((donor == ranking[0]) | (receiver == ranking[0]) | (tallies[receiver] == 0), 0, jnp.maximum(room, 0))
    shifted = jax.random.randint(jax.random.fold_in(own, 4), (amount // 2,), 0, 1 << 20) % (room + 1)
    tallies = tallies.at[donor].add(-shifted).at[receiver].add(shifted)
    members = jnp.searchsorted(jnp.cumsum(tallies), jnp.arange(rows * top), side="right").astype(jnp.int32)
    table = members.reshape(top, rows).T
    table = table[jax.random.permutation(jax.random.fold_in(own, 1), rows)]
    rotation = jax.random.randint(jax.random.fold_in(own, 2), (rows, 1), 0, top)
    return jnp.take_along_axis(table, (jnp.arange(top)[None, :] + rotation) % top, axis=1)


def shares(amount, total, reach, lean, full):
    portions = [(1 << 20) // math.isqrt(grade ** lean) + 1 for grade in range(1, amount + 1)]
    largest = reach if full else min(reach, max(-(-total // amount), total * portions[0] // sum(portions)))
    least = 1 if total - largest >= amount - 1 else 0
    given, rest = [largest] + [least] * (amount - 1), total - largest - least * (amount - 1)
    while rest > 0:
        candidates = [i for i in range(1, amount) if given[i] < largest] or [i for i in range(1, amount) if given[i] < reach]
        mass, left = sum([portions[i] for i in candidates]), rest
        for i in candidates:
            addition = min(reach - given[i], max(1, left * portions[i] // mass), rest)
            given[i] = given[i] + addition
            rest = rest - addition
    return np.array(given)


def gaussian(own_key, shape, scale, bound, shards=(), kind=jnp.bfloat16):
    factor_of = level_of(own_key, shape, shards, -0.22, 0.18) if shards else 1.0
    array = jax.random.normal(own_key, shape, jnp.float32) * scale * factor_of
    return jnp.minimum(jnp.maximum(array, -bound), bound).astype(kind)


def setup_inputs(seed: int = 0) -> dict:
    key_list = jax.random.split(jax.random.key(seed), 9)
    state = gaussian(key_list[0], (NBLK, VARS * LEV, COLS), 1.0, 6.0, ((0, 32),))
    group_of = draw_group_of(jax.random.fold_in(key_list[8], 71), 0)
    w_in = gaussian(key_list[2], (HID, VARS * LEV), (VARS * LEV) ** -0.5, 0.1875)
    w_out = gaussian(key_list[3], (VARS * LEV, HID), HID ** -0.5, 0.1875)
    w_flux = gaussian(key_list[4], (NFLUX, HID), HID ** -0.5, 0.1875)
    owner_keys = jax.random.split(jax.random.fold_in(key_list[5], 1), (NBLK * COLS) // (BLK_DEV * COLS))
    owner_turns = jax.random.permutation(jax.random.fold_in(key_list[5], 3), (NBLK * COLS) // (BLK_DEV * COLS))
    owner = jax.vmap(lambda own, number: shared_out(jax.random.fold_in(key_list[5], 2), own, number, BLK_DEV * COLS, DEVICES, 1, CAP, 2))(owner_keys, owner_turns).reshape((NBLK * COLS, 1))
    ocean_slot = place_ends(jax.random.randint(key_list[6], (NBLK * COLS,), 0, OCN_DEV), jax.random.fold_in(key_list[6], 1), 0, OCN_DEV - 1).astype(jnp.int32)
    remap_weight = jnp.clip(jnp.exp(math.log(4.0) - 2.7725887 * jax.random.uniform(key_list[7], (NBLK * COLS,), jnp.float32) ** level_of(key_list[7], (NBLK * COLS,), ((0, 32),), -0.2, 0.2)), 0.25, 4.0)
    return dict(state=state, group_of=group_of, w_in=w_in, w_out=w_out, w_flux=w_flux, owner=owner, ocean_slot=ocean_slot, remap_weight=remap_weight)


def reference(state, group_of, w_in, w_out, w_flux, owner, ocean_slot, remap_weight):
    group = jnp.zeros_like(state).at[group_of].set(state)

    def one_block(block):
        hidden = jax.nn.silu(jnp.dot(w_in, block, preferred_element_type=jnp.float32)).astype(jnp.bfloat16)
        fresh = (block.astype(jnp.float32) + jnp.dot(w_out, hidden, preferred_element_type=jnp.float32)).astype(jnp.bfloat16)
        surface = jnp.dot(w_flux, hidden, preferred_element_type=jnp.float32)
        return fresh, surface

    new_state, surface = lax.map(one_block, group)
    flux = jnp.transpose(surface, (1, 0, 2)).reshape(NFLUX, NBLK * COLS) * remap_weight[None, :]
    target = owner[:, 0] * OCN_DEV + ocean_slot
    ocean = jnp.zeros((NFLUX, OCEANS), jnp.float32).at[:, target].add(flux)
    return new_state, ocean
```

```python
import functools

import jax
import jax.numpy as jnp
from jax import lax
from jax.experimental import pallas as pl
from jax.experimental.pallas import tpu as pltpu
from jax.sharding import PartitionSpec as P

OCN_DEV = 512
LANES = 256
GROUP = 4
STEP = 256
MIB = 1024 * 1024


def silu(v):
    u = 0.5 * v
    return u + u * jnp.tanh(u)


def side_by_side(blocks):
    return jnp.concatenate([blocks[j] for j in range(GROUP)], axis=1)


def hidden_of(x, w_in, hid, loads=()):
    for i, r in enumerate(range(0, w_in.shape[0], STEP)):
        if loads and i > 0:
            loads[i].wait()
        v = jnp.dot(w_in[r : r + STEP, :], x, preferred_element_type=jnp.float32)
        hid[r : r + STEP, :] = silu(v).astype(jnp.bfloat16)


def updated(buf_in, hid, w_out, buf_out, loads=()):
    cols = buf_in.shape[2]
    h = hid[...]
    for i, r in enumerate(range(0, w_out.shape[0], STEP)):
        if loads:
            loads[i].wait()
        t = jnp.dot(w_out[r : r + STEP, :], h, preferred_element_type=jnp.float32)
        for j in range(GROUP):
            old = buf_in[j, r : r + STEP, :].astype(jnp.float32)
            buf_out[j, r : r + STEP, :] = (old + t[:, j * cols : (j + 1) * cols]).astype(jnp.bfloat16)


def block_copies(hbm, row_of, vmem, sem, g, b, into_vmem):
    copies = []
    for j in range(GROUP):
        there = hbm.at[row_of(g * GROUP + j)]
        src, dst = (there, vmem.at[b, j]) if into_vmem else (vmem.at[b, j], there)
        copies.append(pltpu.make_async_copy(src, dst, sem.at[b, j]))
    return copies


def start(copies):
    for c in copies:
        c.start()


def wait(copies):
    for c in copies:
        c.wait()


def order_kernel(
    nwide, nnarrow, move, table_hbm, owner_hbm, slot_hbm, weight_hbm, order, meta_hbm,
    table, owner, slot, weight, meta, sem,
):
    blocks = owner.shape[0]
    stay = blocks - move
    pairs = [(table_hbm, table), (owner_hbm, owner), (slot_hbm, slot), (weight_hbm, weight)]
    loads = [pltpu.make_async_copy(src, dst, sem.at[i]) for i, (src, dst) in enumerate(pairs)]
    start(loads)
    me = lax.axis_index("wide")
    base = (me * nnarrow + lax.axis_index("narrow")) * blocks
    loads[0].wait()

    def look(s, counts):
        kept, gone = counts
        dest = lax.div(table[base + s], nnarrow * blocks)
        leaves = dest != me
        order[jnp.where(leaves, stay + gone, kept)] = s
        order[blocks + s] = dest
        order[2 * blocks + s] = lax.rem(2 * me - dest + nwide, nwide)
        step = leaves.astype(jnp.int32)
        return kept + 1 - step, gone + step

    lax.fori_loop(0, blocks, look, (jnp.int32(0), jnp.int32(0)))
    wait(loads[1:])
    meta[...] = jnp.zeros_like(meta)
    for k in range(move):
        s = order[stay + k]
        source = order[2 * blocks + s]
        cell = owner[pl.ds(s, 1), :] * OCN_DEV + slot[pl.ds(s, 1), :]
        meta[source, 0:1, :] = cell.astype(jnp.float32)
        meta[source, 1:2, :] = weight[pl.ds(s, 1), :]
    save = pltpu.make_async_copy(meta, meta_hbm, sem.at[len(pairs)])
    save.start()
    save.wait()


def row_parts(src, dst, sem):
    parts = []
    for i, r in enumerate(range(0, src.shape[0], STEP)):
        rows = pl.ds(r, STEP)
        parts.append(pltpu.make_async_copy(src.at[rows], dst.at[rows], sem.at[i]))
    return parts


def leaving_kernel(
    order, state, w_in_hbm, w_out_hbm, w_flux_hbm, out, flux,
    w_in, w_out, w_flux, buf_in, buf_out, hid, sem_w, sem_f, sem_in, sem_out,
):
    blocks, _, cols = state.shape
    move = flux.shape[0]
    stay = blocks - move

    def slot_of(k):
        return order[stay + k]

    def row_of(k):
        return order[blocks + order[stay + k]]

    groups = move // GROUP
    start(block_copies(state, slot_of, buf_in, sem_in, 0, 0, True))
    load_in = row_parts(w_in_hbm, w_in, sem_w.at[0])
    load_out = row_parts(w_out_hbm, w_out, sem_w.at[1])
    load_flux = pltpu.make_async_copy(w_flux_hbm, w_flux, sem_f)
    start(load_in)
    for g in range(groups):
        b = g % 2
        wait(block_copies(state, slot_of, buf_in, sem_in, g, b, True))
        if g == 0:
            load_in[0].wait()
            start(load_out)
            load_flux.start()
        if g + 1 < groups:
            start(block_copies(state, slot_of, buf_in, sem_in, g + 1, 1 - b, True))
        if g >= 2:
            wait(block_copies(out, row_of, buf_out, sem_out, g - 2, b, False))
        hidden_of(side_by_side(buf_in.at[b]), w_in, hid, load_in if g == 0 else ())
        updated(buf_in.at[b], hid, w_out, buf_out.at[b], load_out if g == 0 else ())
        start(block_copies(out, row_of, buf_out, sem_out, g, b, False))
        if g == 0:
            load_flux.wait()
        f = jnp.dot(w_flux[...], hid[...], preferred_element_type=jnp.float32)
        for j in range(GROUP):
            flux[g * GROUP + j] = f[:, j * cols : (j + 1) * cols]
    for g in range(max(groups - 2, 0), groups):
        wait(block_copies(out, row_of, buf_out, sem_out, g, g % 2, False))


def hidden_kernel(
    order, state, w_in_hbm, w_out_hbm, w_flux_hbm, hidden, flux, kept, w_out,
    w_in, w_flux, sem_w, sem_f, sem_kept,
):
    groups, _, _, cols = kept.shape

    def arrivals(g):
        return [
            pltpu.make_async_copy(state.at[order[g * GROUP + j]], kept.at[g, j], sem_kept.at[g, j])
            for j in range(GROUP)
        ]

    load_in = row_parts(w_in_hbm, w_in, sem_w.at[0])
    load_out = row_parts(w_out_hbm, w_out, sem_w.at[1])
    load_flux = pltpu.make_async_copy(w_flux_hbm, w_flux, sem_f)
    start(arrivals(0))
    start(load_in)
    load_flux.start()

    def work(g, loads):
        hidden_of(side_by_side(kept.at[g]), w_in, hidden.at[g], loads)
        if loads:
            load_flux.wait()
        f = jnp.dot(w_flux[...], hidden[g], preferred_element_type=jnp.float32)
        for j in range(GROUP):
            flux[g * GROUP + j] = f[:, j * cols : (j + 1) * cols]

    wait(arrivals(0))
    load_in[0].wait()
    if groups > 1:
        start(arrivals(1))
    work(0, load_in)

    @pl.loop(1, groups)
    def _(g):
        wait(arrivals(g))

        @pl.when(g + 1 < groups)
        def _():
            start(arrivals(g + 1))

        @pl.when(g + 1 == groups)
        def _():
            start(load_out)

        work(g, ())

    if groups == 1:
        start(load_out)
    wait(load_out)


def update_kernel(first, last, order, kept, hidden, w_out, *rest):
    out, buf_out, sem_out = rest[-3:]

    def departures(g):
        return block_copies(out, lambda k: order[k], buf_out, sem_out, g, g - first, False)

    @pl.loop(first, last)
    def _(g):
        updated(kept.at[g], hidden.at[g], w_out, buf_out.at[g - first])
        start(departures(g))

    for g in range(first, last):
        wait(departures(g))


def fill(devices, device, j, f, cell, area, left, right):
    nflux, cols = f.shape
    halves = OCN_DEV // LANES
    bf16 = jnp.bfloat16
    bits = devices.bit_length() - 1
    f = (f * area).astype(bf16)
    apart = (cell // OCN_DEV) ^ device
    far = jnp.zeros_like(apart)
    for i in range(bits):
        far = far | (((apart >> i) & 1) << (bits - 1 - i))
    high = far * halves + (cell % OCN_DEV) // LANES
    low = cell % LANES
    high = jnp.broadcast_to(high.astype(jnp.float32), (nflux, cols)).astype(bf16)
    low = jnp.broadcast_to(low.astype(jnp.float32), (LANES, cols)).astype(bf16)
    rows = lax.broadcasted_iota(jnp.int32, (LANES, cols), 0).astype(jnp.float32).astype(bf16)
    one, zero = jnp.ones((), bf16), jnp.zeros((), bf16)
    right[:, j * cols : (j + 1) * cols] = jnp.where(low == rows, one, zero)
    for h in range(devices * halves):
        left[h * nflux : (h + 1) * nflux, j * cols : (j + 1) * cols] = jnp.where(
            high == jnp.asarray(h, bf16), f, zero
        )


def product(left, right):
    return lax.dot_general(
        left[...], right[...], (((1,), (1,)), ((), ())), preferred_element_type=jnp.float32
    )


def device_index(nnarrow):
    return lax.axis_index("wide") * nnarrow + lax.axis_index("narrow")


def cells_kernel(
    devices, nnarrow, order, flux, flux_away, meta, owner, slot, weight, keep, send, left, right, total
):
    stay, move = flux.shape[0], flux_away.shape[0]
    blocks = stay + move
    device = device_index(nnarrow)
    half = total.shape[0] // 2
    total[...] = jnp.zeros_like(total)

    @pl.loop(0, stay // GROUP, unroll=stay // GROUP if devices <= 32 else 1)
    def _(g):
        b = g % left.shape[0]
        for j in range(GROUP):
            row = pl.ds(order[g * GROUP + j], 1)
            cell = owner[row, :] * OCN_DEV + slot[row, :]
            fill(devices, device, j, flux[g * GROUP + j], cell, weight[row, :], left.at[b], right.at[b])
        total[...] += product(left.at[b], right.at[b])

    for g in range(move // GROUP):
        b = g % left.shape[0]
        for j in range(GROUP):
            k = g * GROUP + j
            dest = order[blocks + order[stay + k]]
            cell = meta[dest, 0:1, :].astype(jnp.int32)
            fill(devices, device, j, flux_away[k], cell, meta[dest, 1:2, :], left.at[b], right.at[b])
        total[...] += product(left.at[b], right.at[b])
    keep[...] = total[:half, :]
    send[...] = total[half:, :].astype(jnp.bfloat16)


def halve_kernel(mine, came, keep, send):
    half = keep.shape[0]
    keep[...] = mine[:half, :] + came[:half, :].astype(jnp.float32)
    send[...] = (mine[half:, :] + came[half:, :].astype(jnp.float32)).astype(jnp.bfloat16)


def last_kernel(mine, came, out):
    nflux = out.shape[0]
    for h in range(OCN_DEV // LANES):
        rows = slice(h * nflux, (h + 1) * nflux)
        out[:, h * LANES : (h + 1) * LANES] = mine[rows, :] + came[rows, :].astype(jnp.float32)


def place_kernel(move, order, arrived, partial, out, sem):
    blocks = out.shape[0]
    stay = blocks - move
    copies = []
    for k in range(move):
        s = order[stay + k]
        copies.append(
            pltpu.make_async_copy(arrived.at[order[2 * blocks + s]], out.at[s], sem.at[k])
        )
    start(copies)
    wait(copies)


SMEM = pl.BlockSpec(memory_space=pltpu.SMEM)
VMEM = pl.BlockSpec(memory_space=pltpu.VMEM)
HBM = pl.BlockSpec(memory_space=pltpu.HBM)
ANY = pl.BlockSpec(memory_space=pl.ANY)


def per_device(state, group_of, w_in, w_out, w_flux, owner, ocean_slot, remap_weight):
    nwide = lax.axis_size("wide")
    nnarrow = lax.axis_size("narrow")
    blocks, depth, cols = state.shape
    inner = w_in.shape[0]
    nflux = w_flux.shape[0]
    devices = nwide * nnarrow
    move = nwide // 2
    stay = blocks - move
    bf16, f32, i32 = jnp.bfloat16, jnp.float32, jnp.int32
    shape = jax.ShapeDtypeStruct
    dma = pltpu.SemaphoreType.DMA
    side = GROUP * cols
    owner = owner[:, 0].reshape(blocks, cols)
    slot = ocean_slot.reshape(blocks, cols)
    weight = remap_weight.reshape(blocks, cols)
    params = pltpu.CompilerParams(vmem_limit_bytes=20 * MIB)
    buffers = 2 if devices <= 32 else 1
    in_hbm = functools.partial(pltpu.with_memory_space_constraint, memory_space=pltpu.HBM)
    in_vmem = functools.partial(pltpu.with_memory_space_constraint, memory_space=pltpu.VMEM)

    def cost(n, products):
        return pl.CostEstimate(
            flops=2 * n * cols * inner * depth * products,
            bytes_accessed=4 * n * depth * cols + 2 * inner * depth * products,
            transcendentals=n * cols * inner,
        )

    def swap(x, axis, bit):
        return lax.ppermute(x, axis, [(i, i ^ bit) for i in range(lax.axis_size(axis))])

    with jax.named_scope("order_of_blocks"):
        order, meta = pl.pallas_call(
            functools.partial(order_kernel, nwide, nnarrow, move),
            out_shape=(shape((3 * blocks,), i32), pltpu.HBM((nwide, 8, cols), f32)),
            in_specs=[HBM] * 4,
            out_specs=(SMEM, HBM),
            scratch_shapes=[
                pltpu.SMEM(group_of.shape, i32),
                pltpu.VMEM((blocks, cols), i32),
                pltpu.VMEM((blocks, cols), i32),
                pltpu.VMEM((blocks, cols), f32),
                pltpu.VMEM((nwide, 8, cols), f32),
                dma((5,)),
            ],
            compiler_params=params,
        )(in_hbm(group_of), in_hbm(owner), in_hbm(slot), in_hbm(weight))
    meta = lax.all_to_all(meta, "wide", split_axis=0, concat_axis=0, tiled=True)

    groups = stay // GROUP
    parts = max(inner, depth) // STEP
    with jax.named_scope("leaving_blocks"):
        outgoing, flux_away = pl.pallas_call(
            leaving_kernel,
            out_shape=(pltpu.HBM((nwide, depth, cols), bf16), shape((move, nflux, cols), f32)),
            in_specs=[SMEM, HBM, HBM, HBM, HBM],
            out_specs=(HBM, VMEM),
            scratch_shapes=[
                pltpu.VMEM((inner, depth), bf16),
                pltpu.VMEM((depth, inner), bf16),
                pltpu.VMEM((nflux, inner), bf16),
                pltpu.VMEM((2, GROUP, depth, cols), bf16),
                pltpu.VMEM((2, GROUP, depth, cols), bf16),
                pltpu.VMEM((inner, side), bf16),
                dma((2, parts)),
                dma,
                dma((2, GROUP)),
                dma((2, GROUP)),
            ],
            compiler_params=params,
            cost_estimate=cost(move, 2),
        )(order, in_hbm(state), in_hbm(w_in), in_hbm(w_out), in_hbm(w_flux))
    outgoing, meta = lax.optimization_barrier((outgoing, meta))
    arrived = lax.all_to_all(outgoing, "wide", split_axis=0, concat_axis=0, tiled=True)

    with jax.named_scope("hidden_of_staying_blocks"):
        hidden, flux, kept, w_out = pl.pallas_call(
            hidden_kernel,
            out_shape=(
                pltpu.VMEM((groups, inner, side), bf16),
                shape((stay, nflux, cols), f32),
                pltpu.VMEM((groups, GROUP, depth, cols), bf16),
                pltpu.VMEM(w_out.shape, bf16),
            ),
            in_specs=[SMEM, HBM, HBM, HBM, HBM],
            out_specs=(VMEM, VMEM, VMEM, VMEM),
            scratch_shapes=[
                pltpu.VMEM((inner, depth), bf16),
                pltpu.VMEM((nflux, inner), bf16),
                dma((2, parts)),
                dma,
                dma((groups, GROUP)),
            ],
            compiler_params=params,
            cost_estimate=cost(stay, 1),
        )(order, in_hbm(state), in_hbm(w_in), in_hbm(w_out), in_hbm(w_flux))

    rows = devices * nflux * OCN_DEV // LANES
    with jax.named_scope("cell_sums"):
        keep, send = pl.pallas_call(
            functools.partial(cells_kernel, devices, nnarrow),
            out_shape=(shape((rows // 2, LANES), f32), shape((rows // 2, LANES), bf16)),
            in_specs=[SMEM] + [VMEM] * 6,
            out_specs=(VMEM, VMEM),
            scratch_shapes=[
                pltpu.VMEM((buffers, rows, side), bf16),
                pltpu.VMEM((buffers, LANES, side), bf16),
                pltpu.VMEM((rows, LANES), f32),
            ],
            compiler_params=pltpu.CompilerParams(vmem_limit_bytes=16 * MIB + 16 * rows * LANES),
            cost_estimate=pl.CostEstimate(
                flops=2 * rows * LANES * blocks * cols, bytes_accessed=6 * rows * LANES, transcendentals=0
            ),
        )(order, flux, flux_away, meta, owner, slot, weight)

    steps = devices.bit_length() - 1
    partial = None
    done = 0

    def update(upto, partial, after):
        begun = () if partial is None else (partial,)
        return pl.pallas_call(
            functools.partial(update_kernel, done, upto),
            out_shape=shape(state.shape, bf16),
            in_specs=[SMEM, VMEM, VMEM, VMEM, ANY] + [ANY] * len(begun),
            out_specs=ANY,
            scratch_shapes=[
                pltpu.VMEM((upto - done, GROUP, depth, cols), bf16),
                dma((upto - done, GROUP)),
            ],
            input_output_aliases={5: 0} if begun else {},
            compiler_params=params,
            cost_estimate=cost((upto - done) * GROUP, 1),
        )(order, in_vmem(kept), in_vmem(hidden), in_vmem(w_out), after, *begun)

    with jax.named_scope("ocean_sums"):
        rows //= 2
        step = 0
        for axis, size in (("narrow", nnarrow), ("wide", nwide)):
            bit = 1
            while bit < size:
                came = swap(send, axis, bit)
                if step > 0:
                    upto = groups if step == steps - 1 else min(groups, done + -(-groups // (steps - 1)))
                    if upto > done:
                        with jax.named_scope("update_of_staying_blocks"):
                            partial = update(upto, partial, keep)
                        done = upto
                if step < steps - 1:
                    rows //= 2
                    keep, send = pl.pallas_call(
                        halve_kernel,
                        out_shape=(shape((rows, LANES), f32), shape((rows, LANES), bf16)),
                        in_specs=[VMEM, VMEM],
                        out_specs=(VMEM, VMEM),
                        compiler_params=params,
                    )(keep, came)
                else:
                    ocean = pl.pallas_call(
                        last_kernel,
                        out_shape=shape((nflux, OCN_DEV), f32),
                        in_specs=[VMEM, VMEM],
                        out_specs=VMEM,
                        compiler_params=params,
                    )(keep, came)
                bit *= 2
                step += 1

    with jax.named_scope("arrived_blocks"):
        new_state = pl.pallas_call(
            functools.partial(place_kernel, move),
            out_shape=shape(state.shape, bf16),
            in_specs=[SMEM, VMEM, ANY],
            out_specs=ANY,
            scratch_shapes=[dma((move,))],
            input_output_aliases={2: 0},
            compiler_params=params,
        )(order, arrived, partial)
    return (new_state, ocean)


def solution(mesh):
    in_specs = (
        P(("wide", "narrow"), None, None),
        P(),
        P(),
        P(),
        P(),
        P(("wide", "narrow"), None),
        P(("wide", "narrow")),
        P(("wide", "narrow")),
    )
    out_specs = (P(("wide", "narrow"), None, None), P(None, ("wide", "narrow")))
    return jax.shard_map(
        per_device, mesh=mesh, in_specs=in_specs, out_specs=out_specs, check_vma=False
    )
```

```python
import functools

import jax
import jax.numpy as jnp
from jax import lax
from jax.experimental import pallas as pl
from jax.experimental.pallas import tpu as pltpu
from jax.sharding import PartitionSpec as P

OCN_DEV = 512
LANES = 256
GROUP = 4
STEP = 256
CHUNK = 512
MIB = 1024 * 1024


def silu(v):
    u = 0.5 * v
    return u + u * jnp.tanh(u)


def side_by_side(blocks):
    return jnp.concatenate([blocks[j] for j in range(GROUP)], axis=1)


def hidden_of(x, w_in, hid, beside=lambda i: None):
    for i, r in enumerate(range(0, w_in.shape[0], STEP)):
        v = jnp.dot(w_in[r : r + STEP, :], x, preferred_element_type=jnp.float32)
        hid[r : r + STEP, :] = silu(v).astype(jnp.bfloat16)
        beside(i)


def updated(buf_in, hid, w_out, buf_out):
    cols = buf_in.shape[2]
    h = hid[...]
    for r in range(0, w_out.shape[0], STEP):
        t = jnp.dot(w_out[r : r + STEP, :], h, preferred_element_type=jnp.float32)
        for j in range(GROUP):
            old = buf_in[j, r : r + STEP, :].astype(jnp.float32)
            buf_out[j, r : r + STEP, :] = (old + t[:, j * cols : (j + 1) * cols]).astype(jnp.bfloat16)


def arrivals_of(hbm, row_of, vmem, sem, g, b):
    return [
        pltpu.make_async_copy(hbm.at[row_of(g * GROUP + j)], vmem.at[b, j], sem.at[b, j])
        for j in range(GROUP)
    ]


def departures(vmem, hbm, row_of, sem, g, b):
    return [
        pltpu.make_async_copy(vmem.at[b, j], hbm.at[row_of(g * GROUP + j)], sem.at[b, j])
        for j in range(GROUP)
    ]


def start(copies):
    for c in copies:
        c.start()


def wait(copies):
    for c in copies:
        c.wait()


def order_kernel(
    nwide, nnarrow, move, table_hbm, owner_hbm, slot_hbm, weight_hbm, order, meta_hbm,
    table, owner, slot, weight, meta, sem,
):
    blocks = owner.shape[0]
    stay = blocks - move
    pairs = [(table_hbm, table), (owner_hbm, owner), (slot_hbm, slot), (weight_hbm, weight)]
    loads = [pltpu.make_async_copy(src, dst, sem.at[i]) for i, (src, dst) in enumerate(pairs)]
    start(loads)
    me = lax.axis_index("wide")
    base = (me * nnarrow + lax.axis_index("narrow")) * blocks
    loads[0].wait()

    def look(s, counts):
        kept, gone = counts
        dest = lax.div(table[base + s], nnarrow * blocks)
        leaves = dest != me
        order[jnp.where(leaves, stay + gone, kept)] = s
        order[blocks + s] = dest
        order[2 * blocks + s] = lax.rem(2 * me - dest + nwide, nwide)
        step = leaves.astype(jnp.int32)
        return kept + 1 - step, gone + step

    lax.fori_loop(0, blocks, look, (jnp.int32(0), jnp.int32(0)))
    wait(loads[1:])
    meta[...] = jnp.zeros_like(meta)
    for k in range(move):
        s = order[stay + k]
        source = order[2 * blocks + s]
        cell = owner[pl.ds(s, 1), :] * OCN_DEV + slot[pl.ds(s, 1), :]
        meta[source, 0:1, :] = cell.astype(jnp.float32)
        meta[source, 1:2, :] = weight[pl.ds(s, 1), :]
    save = pltpu.make_async_copy(meta, meta_hbm, sem.at[len(pairs)])
    save.start()
    save.wait()


def row_parts(src, dst, sem):
    parts = []
    for i, r in enumerate(range(0, src.shape[0], STEP)):
        rows = pl.ds(r, STEP)
        parts.append(pltpu.make_async_copy(src.at[rows], dst.at[rows], sem.at[i]))
    return parts


def leaving_kernel(
    order, state, w_in_hbm, w_out_hbm, w_flux_hbm, out, flux,
    w_in, w_out, w_flux, buf_in, buf_out, hid, sem_w, sem_f, sem_in, sem_out,
):
    blocks, _, cols = state.shape
    move = flux.shape[0]
    stay = blocks - move

    def slot_of(k):
        return order[stay + k]

    def row_of(k):
        return order[blocks + order[stay + k]]

    groups = move // GROUP
    load_in = row_parts(w_in_hbm, w_in, sem_w.at[0])
    load_out = row_parts(w_out_hbm, w_out, sem_w.at[1])
    load_flux = pltpu.make_async_copy(w_flux_hbm, w_flux, sem_f)
    start(arrivals_of(state, slot_of, buf_in, sem_in, 0, 0))
    start(load_in)
    load_flux.start()
    for g in range(groups):
        b = g % 2
        wait(arrivals_of(state, slot_of, buf_in, sem_in, g, b))
        if g == 0:
            wait(load_in)
            start(load_out)
        if g + 1 < groups:
            start(arrivals_of(state, slot_of, buf_in, sem_in, g + 1, 1 - b))
        if g >= 2:
            wait(departures(buf_out, out, row_of, sem_out, g - 2, b))
        hidden_of(side_by_side(buf_in.at[b]), w_in, hid)
        if g == 0:
            wait(load_out)
        updated(buf_in.at[b], hid, w_out, buf_out.at[b])
        start(departures(buf_out, out, row_of, sem_out, g, b))
        if g == 0:
            load_flux.wait()
        f = jnp.dot(w_flux[...], hid[...], preferred_element_type=jnp.float32)
        for j in range(GROUP):
            flux[g * GROUP + j] = f[:, j * cols : (j + 1) * cols]
    for g in range(max(groups - 2, 0), groups):
        wait(departures(buf_out, out, row_of, sem_out, g, g % 2))


def staying_kernel(
    devices, nnarrow,
    order, state, w_in_hbm, w_out_hbm, w_flux_hbm, flux_away_hbm, meta_hbm, owner_hbm, slot_hbm, weight_hbm,
    hidden, kept, w_out, keep, send,
    w_in, w_flux, flux_away, meta, owner, slot, weight, cells, areas, lows, flux, left, right, total,
    sem_w, sem_s, sem_kept,
):
    groups, _, _, cols = kept.shape
    stay = groups * GROUP
    move = flux_away.shape[0]
    blocks = stay + move
    device = lax.axis_index("wide") * nnarrow + lax.axis_index("narrow")

    def arrivals(g):
        return arrivals_of(state, lambda k: order[k], kept, sem_kept, g, g)

    load_in = row_parts(w_in_hbm, w_in, sem_w.at[0])
    load_out = row_parts(w_out_hbm, w_out, sem_w.at[1])
    pairs = [
        (w_flux_hbm, w_flux), (owner_hbm, owner), (slot_hbm, slot), (weight_hbm, weight),
        (flux_away_hbm, flux_away), (meta_hbm, meta),
    ]
    small = [pltpu.make_async_copy(src, dst, sem_s.at[i]) for i, (src, dst) in enumerate(pairs)]
    start(arrivals(0))
    start(load_in)
    start(small)

    def tables():
        for c in range(blocks):
            here = pl.ds(order[c], 1)
            if c < stay:
                cells[c : c + 1, :] = (owner[here, :] * OCN_DEV + slot[here, :]).astype(jnp.float32)
                areas[c : c + 1, :] = weight[here, :]
            else:
                dest = order[blocks + order[c]]
                cells[c : c + 1, :] = meta[dest, 0:1, :]
                areas[c : c + 1, :] = meta[dest, 1:2, :]
        high, low = spread(devices, device, cells[...].astype(jnp.int32))
        cells[...] = high.astype(jnp.float32)
        lows[...] = low.astype(jnp.float32).T

    def factors(c, at, f):
        if isinstance(c, int):
            row, low = slice(c, c + 1), lows[:, c : c + 1]
        else:
            row = pl.ds(c, 1)
            lane = lax.broadcasted_iota(jnp.int32, (cols, blocks), 1)
            low = jnp.sum(jnp.where(lane == c, lows[...], 0.0), axis=1, keepdims=True)
        fill(at, devices * OCN_DEV // LANES, f, areas[row, :], cells[row, :], low, left, right)

    def one_hot(g, j):
        factors(g * GROUP + j, j * cols, flux[j])

    def work(g, beside):
        hidden_of(side_by_side(kept.at[g]), w_in, hidden.at[g], beside)
        f = jnp.dot(w_flux[...], hidden[g], preferred_element_type=jnp.float32)
        for j in range(GROUP):
            flux[j] = f[:, j * cols : (j + 1) * cols]

    wait(arrivals(0))
    wait(load_in)
    if groups > 1:
        start(arrivals(1))
    wait(small)
    tables()
    work(0, lambda i: None)

    def later(g):
        wait(arrivals(g))
        work(g, lambda i: one_hot(g - 1, i) if i < GROUP else None)

    if devices <= 32:
        for g in range(1, groups):
            if g + 1 < groups:
                start(arrivals(g + 1))
            else:
                start(load_out)
            later(g)
            add_product(total, left, right, g == 1)
    else:
        total[...] = jnp.zeros_like(total)

        @pl.loop(1, groups)
        def _(g):
            @pl.when(g + 1 < groups)
            def _():
                start(arrivals(g + 1))

            @pl.when(g + 1 == groups)
            def _():
                start(load_out)

            later(g)
            add_product(total, left, right, False)

    for j in range(GROUP):
        one_hot(groups - 1, j)
    add_product(total, left, right, False)
    for g in range(move // GROUP):
        for j in range(GROUP):
            k = g * GROUP + j
            factors(stay + k, j * cols, flux_away[k])
        add_product(total, left, right, False)
    half = total.shape[0] // 2
    keep[...] = total[:half, :]
    send[...] = total[half:, :].astype(jnp.bfloat16)
    wait(load_out)


def update_kernel(first, last, order, kept, hidden, w_out, *rest):
    out, buf_out, sem_out = rest[-3:]

    def slot_of(k):
        return order[k]

    @pl.loop(first, last)
    def _(g):
        updated(kept.at[g], hidden.at[g], w_out, buf_out.at[g - first])
        start(departures(buf_out, out, slot_of, sem_out, g, g - first))

    for g in range(first, last):
        wait(departures(buf_out, out, slot_of, sem_out, g, g - first))


def spread(devices, device, cell):
    bits = devices.bit_length() - 1
    apart = (cell // OCN_DEV) ^ device
    far = jnp.zeros_like(apart)
    for i in range(bits):
        far = far | (((apart >> i) & 1) << (bits - 1 - i))
    return far * (OCN_DEV // LANES) + cell % OCN_DEV // LANES, cell % LANES


def fill(at, highs, f, area, high, low, left, right):
    nflux, cols = f.shape
    bf16 = jnp.bfloat16
    f = (f * area).astype(bf16)
    high = jnp.broadcast_to(high, (nflux, cols)).astype(bf16)
    low = jnp.broadcast_to(low, (cols, LANES)).astype(bf16)
    lanes = lax.broadcasted_iota(jnp.int32, (cols, LANES), 1).astype(jnp.float32).astype(bf16)
    one, zero = jnp.ones((), bf16), jnp.zeros((), bf16)
    right[at : at + cols, :] = jnp.where(low == lanes, one, zero)
    for h in range(highs):
        left[h * nflux : (h + 1) * nflux, at : at + cols] = jnp.where(
            high == jnp.asarray(h, bf16), f, zero
        )


def add_product(total, left, right, first):
    h = right[...]
    for r in range(0, total.shape[0], CHUNK):
        p = jnp.dot(left[r : r + CHUNK, :], h, preferred_element_type=jnp.float32)
        total[r : r + CHUNK, :] = p if first else total[r : r + CHUNK, :] + p


def halve_kernel(mine, came, keep, *sends):
    rows = keep.shape[0]
    keep[...] = mine[:rows, :] + came[:rows, :].astype(jnp.float32)
    for i, send in enumerate(sends):
        at = pl.ds((i + 1) * rows, rows)
        send[...] = (mine[at, :] + came[at, :].astype(jnp.float32)).astype(jnp.bfloat16)


def last_kernel(move, order, arrived, mine, *rest):
    came, (_, out, ocean, sem) = rest[:-4], rest[-4:]
    blocks = out.shape[0]
    stay = blocks - move
    copies = []
    for k in range(move):
        s = order[stay + k]
        copies.append(
            pltpu.make_async_copy(arrived.at[order[2 * blocks + s]], out.at[s], sem.at[k])
        )
    start(copies)
    nflux = ocean.shape[0]
    for h in range(OCN_DEV // LANES):
        rows = slice(h * nflux, (h + 1) * nflux)
        part = mine[rows, :]
        for c in came:
            part = part + c[rows, :].astype(jnp.float32)
        ocean[:, h * LANES : (h + 1) * LANES] = part
    wait(copies)


SMEM = pl.BlockSpec(memory_space=pltpu.SMEM)
VMEM = pl.BlockSpec(memory_space=pltpu.VMEM)
HBM = pl.BlockSpec(memory_space=pltpu.HBM)
ANY = pl.BlockSpec(memory_space=pl.ANY)


def per_device(state, group_of, w_in, w_out, w_flux, owner, ocean_slot, remap_weight):
    nwide = lax.axis_size("wide")
    nnarrow = lax.axis_size("narrow")
    blocks, depth, cols = state.shape
    inner = w_in.shape[0]
    nflux = w_flux.shape[0]
    devices = nwide * nnarrow
    move = nwide // 2
    stay = blocks - move
    bf16, f32, i32 = jnp.bfloat16, jnp.float32, jnp.int32
    shape = jax.ShapeDtypeStruct
    dma = pltpu.SemaphoreType.DMA
    side = GROUP * cols
    owner = owner[:, 0].reshape(blocks, cols)
    slot = ocean_slot.reshape(blocks, cols)
    weight = remap_weight.reshape(blocks, cols)
    params = pltpu.CompilerParams(vmem_limit_bytes=20 * MIB)
    in_hbm = functools.partial(pltpu.with_memory_space_constraint, memory_space=pltpu.HBM)
    in_vmem = functools.partial(pltpu.with_memory_space_constraint, memory_space=pltpu.VMEM)

    def cost(n, products):
        return pl.CostEstimate(
            flops=2 * n * cols * inner * depth * products,
            bytes_accessed=4 * n * depth * cols + 2 * inner * depth * products,
            transcendentals=n * cols * inner,
        )

    def swap(x, axis, bit):
        return lax.ppermute(x, axis, [(i, i ^ bit) for i in range(lax.axis_size(axis))])

    with jax.named_scope("order_of_blocks"):
        order, meta = pl.pallas_call(
            functools.partial(order_kernel, nwide, nnarrow, move),
            out_shape=(shape((3 * blocks,), i32), pltpu.HBM((nwide, 8, cols), f32)),
            in_specs=[HBM] * 4,
            out_specs=(SMEM, HBM),
            scratch_shapes=[
                pltpu.SMEM(group_of.shape, i32),
                pltpu.VMEM((blocks, cols), i32),
                pltpu.VMEM((blocks, cols), i32),
                pltpu.VMEM((blocks, cols), f32),
                pltpu.VMEM((nwide, 8, cols), f32),
                dma((5,)),
            ],
            compiler_params=params,
        )(in_hbm(group_of), in_hbm(owner), in_hbm(slot), in_hbm(weight))
    meta = lax.all_to_all(meta, "wide", split_axis=0, concat_axis=0, tiled=True)

    groups = stay // GROUP
    parts = max(inner, depth) // STEP
    with jax.named_scope("leaving_blocks"):
        outgoing, flux_away = pl.pallas_call(
            leaving_kernel,
            out_shape=(pltpu.HBM((nwide, depth, cols), bf16), pltpu.HBM((move, nflux, cols), f32)),
            in_specs=[SMEM, HBM, HBM, HBM, HBM],
            out_specs=(HBM, VMEM),
            scratch_shapes=[
                pltpu.VMEM((inner, depth), bf16),
                pltpu.VMEM((depth, inner), bf16),
                pltpu.VMEM((nflux, inner), bf16),
                pltpu.VMEM((2, GROUP, depth, cols), bf16),
                pltpu.VMEM((2, GROUP, depth, cols), bf16),
                pltpu.VMEM((inner, side), bf16),
                dma((2, parts)),
                dma,
                dma((2, GROUP)),
                dma((2, GROUP)),
            ],
            compiler_params=params,
            cost_estimate=cost(move, 2),
        )(order, in_hbm(state), in_hbm(w_in), in_hbm(w_out), in_hbm(w_flux))
    outgoing, meta = lax.optimization_barrier((outgoing, meta))
    arrived = lax.all_to_all(outgoing, "wide", split_axis=0, concat_axis=0, tiled=True)

    rows = devices * nflux * OCN_DEV // LANES
    with jax.named_scope("staying_blocks_and_cell_sums"):
        hidden, kept, w_out, keep, send = pl.pallas_call(
            functools.partial(staying_kernel, devices, nnarrow),
            out_shape=(
                pltpu.VMEM((groups, inner, side), bf16),
                pltpu.VMEM((groups, GROUP, depth, cols), bf16),
                pltpu.VMEM(w_out.shape, bf16),
                shape((rows // 2, LANES), f32),
                shape((rows // 2, LANES), bf16),
            ),
            in_specs=[SMEM] + [HBM] * 9,
            out_specs=(VMEM,) * 5,
            scratch_shapes=[
                pltpu.VMEM((inner, depth), bf16),
                pltpu.VMEM((nflux, inner), bf16),
                pltpu.VMEM((move, nflux, cols), f32),
                pltpu.VMEM((nwide, 8, cols), f32),
                pltpu.VMEM((blocks, cols), i32),
                pltpu.VMEM((blocks, cols), i32),
                pltpu.VMEM((blocks, cols), f32),
                pltpu.VMEM((blocks, cols), f32),
                pltpu.VMEM((blocks, cols), f32),
                pltpu.VMEM((cols, blocks), f32),
                pltpu.VMEM((GROUP, nflux, cols), f32),
                pltpu.VMEM((rows, side), bf16),
                pltpu.VMEM((side, LANES), bf16),
                pltpu.VMEM((rows, LANES), f32),
                dma((2, parts)),
                dma((6,)),
                dma((groups, GROUP)),
            ],
            compiler_params=pltpu.CompilerParams(vmem_limit_bytes=20 * MIB + 14 * rows * LANES),
            cost_estimate=pl.CostEstimate(
                flops=2 * cols * (stay * inner * depth + rows * LANES * blocks),
                bytes_accessed=2 * stay * depth * cols + 4 * inner * depth,
                transcendentals=stay * cols * inner,
            ),
        )(
            order,
            *map(in_hbm, (state, w_in, w_out, w_flux, flux_away, meta, owner, slot, weight)),
        )

    partial = None
    done = 0

    def update(upto, partial, after):
        begun = () if partial is None else (partial,)
        return pl.pallas_call(
            functools.partial(update_kernel, done, upto),
            out_shape=shape(state.shape, bf16),
            in_specs=[SMEM, VMEM, VMEM, VMEM, ANY] + [ANY] * len(begun),
            out_specs=ANY,
            scratch_shapes=[
                pltpu.VMEM((upto - done, GROUP, depth, cols), bf16),
                dma((upto - done, GROUP)),
            ],
            input_output_aliases={5: 0} if begun else {},
            compiler_params=params,
            cost_estimate=cost((upto - done) * GROUP, 1),
        )(order, in_vmem(kept), in_vmem(hidden), in_vmem(w_out), after, *begun)

    bits = [("narrow", 1 << i) for i in range(nnarrow.bit_length() - 1)]
    bits += [("wide", 1 << i) for i in range(nwide.bit_length() - 3)]
    own = nflux * OCN_DEV // LANES
    rows //= 2
    sends = (send,)
    with jax.named_scope("ocean_sums"):
        for i, (axis, bit) in enumerate(bits):
            came = swap(sends[0], axis, bit)
            if i > 0:
                upto = min(groups, done + -(-groups // len(bits)))
                if upto > done:
                    with jax.named_scope("update_of_staying_blocks"):
                        partial = update(upto, partial, keep)
                    done = upto
            quarters = i == len(bits) - 1
            rows = own if quarters else rows // 2
            count = 3 if quarters else 1
            keep, *sends = pl.pallas_call(
                halve_kernel,
                out_shape=(shape((rows, LANES), f32),) + (shape((rows, LANES), bf16),) * count,
                in_specs=[VMEM, VMEM],
                out_specs=(VMEM,) * (1 + count),
                compiler_params=params,
            )(keep, came)
        came = [swap(x, "wide", d * nwide // 4) for x, d in zip(sends, (2, 1, 3))]
        with jax.named_scope("update_of_staying_blocks"):
            partial = update(groups, partial, keep)

    with jax.named_scope("arrived_blocks_and_last_sums"):
        new_state, ocean = pl.pallas_call(
            functools.partial(last_kernel, move),
            out_shape=(shape(state.shape, bf16), shape((nflux, OCN_DEV), f32)),
            in_specs=[SMEM] + [VMEM] * 5 + [ANY],
            out_specs=(ANY, VMEM),
            scratch_shapes=[dma((move,))],
            input_output_aliases={6: 0},
            compiler_params=params,
        )(order, arrived, keep, *came, partial)
    return (new_state, ocean)


def solution(mesh):
    in_specs = (
        P(("wide", "narrow"), None, None),
        P(),
        P(),
        P(),
        P(),
        P(("wide", "narrow"), None),
        P(("wide", "narrow")),
        P(("wide", "narrow")),
    )
    out_specs = (P(("wide", "narrow"), None, None), P(None, ("wide", "narrow")))
    return jax.shard_map(
        per_device, mesh=mesh, in_specs=in_specs, out_specs=out_specs, check_vma=False
    )
```

```python
import functools

import jax
import jax.numpy as jnp
from jax import lax
from jax.experimental import pallas as pl
from jax.experimental.pallas import tpu as pltpu
from jax.sharding import PartitionSpec as P

OCN_DEV = 512
LANES = 256
GROUP = 4
STEP = 256
CHUNK = 512
MIB = 1024 * 1024


def silu(v):
    u = 0.5 * v
    return u + u * jnp.tanh(u)


def side_by_side(blocks):
    return jnp.concatenate([blocks[j] for j in range(GROUP)], axis=1)


def hidden_of(x, w_in, hid, beside=lambda i: None):
    for i, r in enumerate(range(0, w_in.shape[0], STEP)):
        v = jnp.dot(w_in[r : r + STEP, :], x, preferred_element_type=jnp.float32)
        hid[r : r + STEP, :] = silu(v).astype(jnp.bfloat16)
        beside(i)


def updated(buf_in, hid, w_out, buf_out):
    cols = buf_in.shape[2]
    h = hid[...]
    for r in range(0, w_out.shape[0], STEP):
        t = jnp.dot(w_out[r : r + STEP, :], h, preferred_element_type=jnp.float32)
        for j in range(GROUP):
            old = buf_in[j, r : r + STEP, :].astype(jnp.float32)
            buf_out[j, r : r + STEP, :] = (old + t[:, j * cols : (j + 1) * cols]).astype(jnp.bfloat16)


def arrivals_of(hbm, row_of, vmem, sem, g, b):
    return [
        pltpu.make_async_copy(hbm.at[row_of(g * GROUP + j)], vmem.at[b, j], sem.at[b, j])
        for j in range(GROUP)
    ]


def departures(vmem, hbm, row_of, sem, g, b):
    return [
        pltpu.make_async_copy(vmem.at[b, j], hbm.at[row_of(g * GROUP + j)], sem.at[b, j])
        for j in range(GROUP)
    ]


def start(copies):
    for c in copies:
        c.start()


def wait(copies):
    for c in copies:
        c.wait()


def order_kernel(
    nwide, nnarrow, move, table_hbm, owner_hbm, slot_hbm, weight_hbm, order, meta_hbm,
    table, owner, slot, weight, meta, sem,
):
    blocks = owner.shape[0]
    stay = blocks - move
    pairs = [(table_hbm, table), (owner_hbm, owner), (slot_hbm, slot), (weight_hbm, weight)]
    loads = [pltpu.make_async_copy(src, dst, sem.at[i]) for i, (src, dst) in enumerate(pairs)]
    start(loads)
    me = lax.axis_index("wide")
    base = (me * nnarrow + lax.axis_index("narrow")) * blocks
    loads[0].wait()

    def look(s, counts):
        kept, gone = counts
        dest = lax.div(table[base + s], nnarrow * blocks)
        leaves = dest != me
        order[jnp.where(leaves, stay + gone, kept)] = s
        order[blocks + s] = dest
        order[2 * blocks + s] = lax.rem(2 * me - dest + nwide, nwide)
        step = leaves.astype(jnp.int32)
        return kept + 1 - step, gone + step

    lax.fori_loop(0, blocks, look, (jnp.int32(0), jnp.int32(0)))
    wait(loads[1:])
    meta[...] = jnp.zeros_like(meta)
    for k in range(move):
        s = order[stay + k]
        source = order[2 * blocks + s]
        cell = owner[pl.ds(s, 1), :] * OCN_DEV + slot[pl.ds(s, 1), :]
        meta[source, 0:1, :] = cell.astype(jnp.float32)
        meta[source, 1:2, :] = weight[pl.ds(s, 1), :]
    save = pltpu.make_async_copy(meta, meta_hbm, sem.at[len(pairs)])
    save.start()
    save.wait()


def row_parts(src, dst, sem):
    parts = []
    for i, r in enumerate(range(0, src.shape[0], STEP)):
        rows = pl.ds(r, STEP)
        parts.append(pltpu.make_async_copy(src.at[rows], dst.at[rows], sem.at[i]))
    return parts


def leaving_kernel(
    order, state, w_in_hbm, w_out_hbm, w_flux_hbm, out, flux,
    w_in, w_out, w_flux, buf_in, buf_out, hid, sem_w, sem_f, sem_in, sem_out,
):
    blocks, _, cols = state.shape
    move = flux.shape[0]
    stay = blocks - move

    def slot_of(k):
        return order[stay + k]

    def row_of(k):
        return order[blocks + order[stay + k]]

    groups = move // GROUP
    load_in = row_parts(w_in_hbm, w_in, sem_w.at[0])
    load_out = row_parts(w_out_hbm, w_out, sem_w.at[1])
    load_flux = pltpu.make_async_copy(w_flux_hbm, w_flux, sem_f)
    start(arrivals_of(state, slot_of, buf_in, sem_in, 0, 0))
    start(load_in)
    load_flux.start()
    for g in range(groups):
        b = g % 2
        wait(arrivals_of(state, slot_of, buf_in, sem_in, g, b))
        if g == 0:
            wait(load_in)
            start(load_out)
        if g + 1 < groups:
            start(arrivals_of(state, slot_of, buf_in, sem_in, g + 1, 1 - b))
        if g >= 2:
            wait(departures(buf_out, out, row_of, sem_out, g - 2, b))
        hidden_of(side_by_side(buf_in.at[b]), w_in, hid)
        if g == 0:
            wait(load_out)
        updated(buf_in.at[b], hid, w_out, buf_out.at[b])
        start(departures(buf_out, out, row_of, sem_out, g, b))
        if g == 0:
            load_flux.wait()
        f = jnp.dot(w_flux[...], hid[...], preferred_element_type=jnp.float32)
        for j in range(GROUP):
            flux[g * GROUP + j] = f[:, j * cols : (j + 1) * cols]
    for g in range(max(groups - 2, 0), groups):
        wait(departures(buf_out, out, row_of, sem_out, g, g % 2))


def staying_kernel(
    devices, nnarrow,
    order, state, w_in_hbm, w_out_hbm, w_flux_hbm, flux_away_hbm, meta_hbm, owner_hbm, slot_hbm, weight_hbm,
    hidden, kept, w_out, keep, send,
    w_in, w_flux, flux_away, meta, owner, slot, weight, cells, areas, lows, flux, left, right, total,
    sem_w, sem_s, sem_kept,
):
    groups, _, _, cols = kept.shape
    stay = groups * GROUP
    move = flux_away.shape[0]
    blocks = stay + move
    device = lax.axis_index("wide") * nnarrow + lax.axis_index("narrow")

    def arrivals(g):
        return arrivals_of(state, lambda k: order[k], kept, sem_kept, g, g)

    load_in = row_parts(w_in_hbm, w_in, sem_w.at[0])
    load_out = row_parts(w_out_hbm, w_out, sem_w.at[1])
    pairs = [
        (w_flux_hbm, w_flux), (owner_hbm, owner), (slot_hbm, slot), (weight_hbm, weight),
        (flux_away_hbm, flux_away), (meta_hbm, meta),
    ]
    small = [pltpu.make_async_copy(src, dst, sem_s.at[i]) for i, (src, dst) in enumerate(pairs)]
    start(arrivals(0))
    start(load_in)
    start(small)

    def tables():
        for c in range(blocks):
            here = pl.ds(order[c], 1)
            if c < stay:
                cells[c : c + 1, :] = (owner[here, :] * OCN_DEV + slot[here, :]).astype(jnp.float32)
                areas[c : c + 1, :] = weight[here, :]
            else:
                dest = order[blocks + order[c]]
                cells[c : c + 1, :] = meta[dest, 0:1, :]
                areas[c : c + 1, :] = meta[dest, 1:2, :]
        high, low = spread(devices, device, cells[...].astype(jnp.int32))
        cells[...] = high.astype(jnp.float32)
        lows[...] = low.astype(jnp.float32).T

    def factors(c, at, f):
        if isinstance(c, int):
            row, low = slice(c, c + 1), lows[:, c : c + 1]
        else:
            row = pl.ds(c, 1)
            lane = lax.broadcasted_iota(jnp.int32, (cols, blocks), 1)
            low = jnp.sum(jnp.where(lane == c, lows[...], 0.0), axis=1, keepdims=True)
        fill(at, devices * OCN_DEV // LANES, f, areas[row, :], cells[row, :], low, left, right)

    def one_hot(g, j):
        factors(g * GROUP + j, j * cols, flux[j])

    def work(g, beside):
        hidden_of(side_by_side(kept.at[g]), w_in, hidden.at[g], beside)
        f = jnp.dot(w_flux[...], hidden[g], preferred_element_type=jnp.float32)
        for j in range(GROUP):
            flux[j] = f[:, j * cols : (j + 1) * cols]

    wait(arrivals(0))
    wait(load_in)
    if groups > 1:
        start(arrivals(1))
    wait(small)
    tables()
    work(0, lambda i: None)

    def later(g):
        wait(arrivals(g))
        work(g, lambda i: one_hot(g - 1, i) if i < GROUP else None)

    if devices <= 32:
        for g in range(1, groups):
            if g + 1 < groups:
                start(arrivals(g + 1))
            else:
                start(load_out)
            later(g)
            add_product(total, left, right, g == 1)
    else:
        total[...] = jnp.zeros_like(total)

        @pl.loop(1, groups)
        def _(g):
            @pl.when(g + 1 < groups)
            def _():
                start(arrivals(g + 1))

            @pl.when(g + 1 == groups)
            def _():
                start(load_out)

            later(g)
            add_product(total, left, right, False)

    for j in range(GROUP):
        one_hot(groups - 1, j)
    add_product(total, left, right, False)
    for g in range(move // GROUP):
        for j in range(GROUP):
            k = g * GROUP + j
            factors(stay + k, j * cols, flux_away[k])
        add_product(total, left, right, False)
    half = total.shape[0] // 2
    keep[...] = total[:half, :]
    send[...] = total[half:, :].astype(jnp.bfloat16)
    wait(load_out)


def update_kernel(first, last, order, kept, hidden, w_out, *rest):
    out, buf_out, sem_out = rest[-3:]

    def slot_of(k):
        return order[k]

    @pl.loop(first, last)
    def _(g):
        updated(kept.at[g], hidden.at[g], w_out, buf_out.at[g - first])
        start(departures(buf_out, out, slot_of, sem_out, g, g - first))

    for g in range(first, last):
        wait(departures(buf_out, out, slot_of, sem_out, g, g - first))


def spread(devices, device, cell):
    bits = devices.bit_length() - 1
    apart = (cell // OCN_DEV) ^ device
    far = jnp.zeros_like(apart)
    for i in range(bits):
        far = far | (((apart >> i) & 1) << (bits - 1 - i))
    return far * (OCN_DEV // LANES) + cell % OCN_DEV // LANES, cell % LANES


def fill(at, highs, f, area, high, low, left, right):
    nflux, cols = f.shape
    bf16 = jnp.bfloat16
    f = (f * area).astype(bf16)
    high = jnp.broadcast_to(high, (nflux, cols)).astype(bf16)
    low = jnp.broadcast_to(low, (cols, LANES)).astype(bf16)
    lanes = lax.broadcasted_iota(jnp.int32, (cols, LANES), 1).astype(jnp.float32).astype(bf16)
    one, zero = jnp.ones((), bf16), jnp.zeros((), bf16)
    right[at : at + cols, :] = jnp.where(low == lanes, one, zero)
    for h in range(highs):
        left[h * nflux : (h + 1) * nflux, at : at + cols] = jnp.where(
            high == jnp.asarray(h, bf16), f, zero
        )


def add_product(total, left, right, first):
    h = right[...]
    for r in range(0, total.shape[0], CHUNK):
        p = jnp.dot(left[r : r + CHUNK, :], h, preferred_element_type=jnp.float32)
        total[r : r + CHUNK, :] = p if first else total[r : r + CHUNK, :] + p


def halve_kernel(mine, came, keep, *sends):
    rows = keep.shape[0]
    keep[...] = mine[:rows, :] + came[:rows, :].astype(jnp.float32)
    for i, send in enumerate(sends):
        at = pl.ds((i + 1) * rows, rows)
        send[...] = (mine[at, :] + came[at, :].astype(jnp.float32)).astype(jnp.bfloat16)


def place_kernel(move, order, arrived, _, out, sem):
    blocks = out.shape[0]
    stay = blocks - move
    copies = []
    for k in range(move):
        s = order[stay + k]
        copies.append(
            pltpu.make_async_copy(arrived.at[order[2 * blocks + s]], out.at[s], sem.at[k])
        )
    start(copies)
    wait(copies)


def last_kernel(mine, *rest):
    came, ocean = rest[:-2], rest[-1]
    nflux = ocean.shape[0]
    for h in range(OCN_DEV // LANES):
        rows = slice(h * nflux, (h + 1) * nflux)
        part = mine[rows, :]
        for c in came:
            part = part + c[rows, :].astype(jnp.float32)
        ocean[:, h * LANES : (h + 1) * LANES] = part


SMEM = pl.BlockSpec(memory_space=pltpu.SMEM)
VMEM = pl.BlockSpec(memory_space=pltpu.VMEM)
HBM = pl.BlockSpec(memory_space=pltpu.HBM)
ANY = pl.BlockSpec(memory_space=pl.ANY)


def per_device(state, group_of, w_in, w_out, w_flux, owner, ocean_slot, remap_weight):
    nwide = lax.axis_size("wide")
    nnarrow = lax.axis_size("narrow")
    blocks, depth, cols = state.shape
    inner = w_in.shape[0]
    nflux = w_flux.shape[0]
    devices = nwide * nnarrow
    move = nwide // 2
    stay = blocks - move
    bf16, f32, i32 = jnp.bfloat16, jnp.float32, jnp.int32
    shape = jax.ShapeDtypeStruct
    dma = pltpu.SemaphoreType.DMA
    side = GROUP * cols
    owner = owner[:, 0].reshape(blocks, cols)
    slot = ocean_slot.reshape(blocks, cols)
    weight = remap_weight.reshape(blocks, cols)
    params = pltpu.CompilerParams(vmem_limit_bytes=20 * MIB)
    in_hbm = functools.partial(pltpu.with_memory_space_constraint, memory_space=pltpu.HBM)
    in_vmem = functools.partial(pltpu.with_memory_space_constraint, memory_space=pltpu.VMEM)

    def cost(n, products):
        return pl.CostEstimate(
            flops=2 * n * cols * inner * depth * products,
            bytes_accessed=4 * n * depth * cols + 2 * inner * depth * products,
            transcendentals=n * cols * inner,
        )

    def swap(x, axis, bit):
        return lax.ppermute(x, axis, [(i, i ^ bit) for i in range(lax.axis_size(axis))])

    with jax.named_scope("order_of_blocks"):
        order, meta = pl.pallas_call(
            functools.partial(order_kernel, nwide, nnarrow, move),
            out_shape=(shape((3 * blocks,), i32), pltpu.HBM((nwide, 8, cols), f32)),
            in_specs=[HBM] * 4,
            out_specs=(SMEM, HBM),
            scratch_shapes=[
                pltpu.SMEM(group_of.shape, i32),
                pltpu.VMEM((blocks, cols), i32),
                pltpu.VMEM((blocks, cols), i32),
                pltpu.VMEM((blocks, cols), f32),
                pltpu.VMEM((nwide, 8, cols), f32),
                dma((5,)),
            ],
            compiler_params=params,
        )(in_hbm(group_of), in_hbm(owner), in_hbm(slot), in_hbm(weight))
    meta = lax.all_to_all(meta, "wide", split_axis=0, concat_axis=0, tiled=True)

    groups = stay // GROUP
    parts = max(inner, depth) // STEP
    with jax.named_scope("leaving_blocks"):
        outgoing, flux_away = pl.pallas_call(
            leaving_kernel,
            out_shape=(pltpu.HBM((nwide, depth, cols), bf16), pltpu.HBM((move, nflux, cols), f32)),
            in_specs=[SMEM, HBM, HBM, HBM, HBM],
            out_specs=(HBM, VMEM),
            scratch_shapes=[
                pltpu.VMEM((inner, depth), bf16),
                pltpu.VMEM((depth, inner), bf16),
                pltpu.VMEM((nflux, inner), bf16),
                pltpu.VMEM((2, GROUP, depth, cols), bf16),
                pltpu.VMEM((2, GROUP, depth, cols), bf16),
                pltpu.VMEM((inner, side), bf16),
                dma((2, parts)),
                dma,
                dma((2, GROUP)),
                dma((2, GROUP)),
            ],
            compiler_params=params,
            cost_estimate=cost(move, 2),
        )(order, in_hbm(state), in_hbm(w_in), in_hbm(w_out), in_hbm(w_flux))
    outgoing, meta = lax.optimization_barrier((outgoing, meta))
    arrived = lax.all_to_all(outgoing, "wide", split_axis=0, concat_axis=0, tiled=True)

    rows = devices * nflux * OCN_DEV // LANES
    with jax.named_scope("staying_blocks_and_cell_sums"):
        hidden, kept, w_out, keep, send = pl.pallas_call(
            functools.partial(staying_kernel, devices, nnarrow),
            out_shape=(
                pltpu.VMEM((groups, inner, side), bf16),
                pltpu.VMEM((groups, GROUP, depth, cols), bf16),
                pltpu.VMEM(w_out.shape, bf16),
                shape((rows // 2, LANES), f32),
                shape((rows // 2, LANES), bf16),
            ),
            in_specs=[SMEM] + [HBM] * 9,
            out_specs=(VMEM,) * 5,
            scratch_shapes=[
                pltpu.VMEM((inner, depth), bf16),
                pltpu.VMEM((nflux, inner), bf16),
                pltpu.VMEM((move, nflux, cols), f32),
                pltpu.VMEM((nwide, 8, cols), f32),
                pltpu.VMEM((blocks, cols), i32),
                pltpu.VMEM((blocks, cols), i32),
                pltpu.VMEM((blocks, cols), f32),
                pltpu.VMEM((blocks, cols), f32),
                pltpu.VMEM((blocks, cols), f32),
                pltpu.VMEM((cols, blocks), f32),
                pltpu.VMEM((GROUP, nflux, cols), f32),
                pltpu.VMEM((rows, side), bf16),
                pltpu.VMEM((side, LANES), bf16),
                pltpu.VMEM((rows, LANES), f32),
                dma((2, parts)),
                dma((6,)),
                dma((groups, GROUP)),
            ],
            compiler_params=pltpu.CompilerParams(vmem_limit_bytes=20 * MIB + 14 * rows * LANES),
            cost_estimate=pl.CostEstimate(
                flops=2 * cols * (stay * inner * depth + rows * LANES * blocks),
                bytes_accessed=2 * stay * depth * cols + 4 * inner * depth,
                transcendentals=stay * cols * inner,
            ),
        )(
            order,
            *map(in_hbm, (state, w_in, w_out, w_flux, flux_away, meta, owner, slot, weight)),
        )

    partial = None
    done = 0

    def update(upto, partial, after):
        begun = () if partial is None else (partial,)
        return pl.pallas_call(
            functools.partial(update_kernel, done, upto),
            out_shape=shape(state.shape, bf16),
            in_specs=[SMEM, VMEM, VMEM, VMEM, ANY] + [ANY] * len(begun),
            out_specs=ANY,
            scratch_shapes=[
                pltpu.VMEM((upto - done, GROUP, depth, cols), bf16),
                dma((upto - done, GROUP)),
            ],
            input_output_aliases={5: 0} if begun else {},
            compiler_params=params,
            cost_estimate=cost((upto - done) * GROUP, 1),
        )(order, in_vmem(kept), in_vmem(hidden), in_vmem(w_out), after, *begun)

    bits = [("narrow", 1 << i) for i in range(nnarrow.bit_length() - 1)]
    bits += [("wide", 1 << i) for i in range(nwide.bit_length() - 3)]
    own = nflux * OCN_DEV // LANES
    rows //= 2
    sends = (send,)
    with jax.named_scope("ocean_sums"):
        for i, (axis, bit) in enumerate(bits):
            came = swap(sends[0], axis, bit)
            if i > 0:
                upto = min(groups, done + -(-groups // len(bits)))
                if upto > done:
                    with jax.named_scope("update_of_staying_blocks"):
                        partial = update(upto, partial, keep)
                    done = upto
            quarters = i == len(bits) - 1
            rows = own if quarters else rows // 2
            count = 3 if quarters else 1
            keep, *sends = pl.pallas_call(
                halve_kernel,
                out_shape=(shape((rows, LANES), f32),) + (shape((rows, LANES), bf16),) * count,
                in_specs=[VMEM, VMEM],
                out_specs=(VMEM,) * (1 + count),
                compiler_params=params,
            )(keep, came)
        came = [swap(x, "wide", d * nwide // 4) for x, d in zip(sends, (2, 1, 3))]
        with jax.named_scope("update_of_staying_blocks"):
            partial = update(groups, partial, keep)

    with jax.named_scope("arrived_blocks"):
        new_state = pl.pallas_call(
            functools.partial(place_kernel, move),
            out_shape=shape(state.shape, bf16),
            in_specs=[SMEM, VMEM, ANY],
            out_specs=ANY,
            scratch_shapes=[dma((move,))],
            input_output_aliases={2: 0},
            compiler_params=params,
        )(order, arrived, partial)
    with jax.named_scope("last_sums"):
        ocean = pl.pallas_call(
            last_kernel,
            out_shape=shape((nflux, OCN_DEV), f32),
            in_specs=[VMEM] * 4 + [ANY],
            out_specs=VMEM,
            compiler_params=params,
        )(keep, *came, new_state)
    return (new_state, ocean)


def solution(mesh):
    in_specs = (
        P(("wide", "narrow"), None, None),
        P(),
        P(),
        P(),
        P(),
        P(("wide", "narrow"), None),
        P(("wide", "narrow")),
        P(("wide", "narrow")),
    )
    out_specs = (P(("wide", "narrow"), None, None), P(None, ("wide", "narrow")))
    return jax.shard_map(
        per_device, mesh=mesh, in_specs=in_specs, out_specs=out_specs, check_vma=False
    )
```

```python
import functools

import jax
import jax.numpy as jnp
from jax import lax
from jax.experimental import pallas as pl
from jax.experimental.pallas import tpu as pltpu
from jax.sharding import PartitionSpec as P

OCN_DEV = 512
LANES = 256
GROUP = 4
STEP = 256
CHUNK = 512
MIB = 1024 * 1024


def silu(v):
    u = 0.5 * v
    return u + u * jnp.tanh(u)


def side_by_side(blocks):
    return jnp.concatenate([blocks[j] for j in range(GROUP)], axis=1)


def hidden_of(x, w_in, hid, beside=lambda i: None):
    for i, r in enumerate(range(0, w_in.shape[0], STEP)):
        v = jnp.dot(w_in[r : r + STEP, :], x, preferred_element_type=jnp.float32)
        hid[r : r + STEP, :] = silu(v).astype(jnp.bfloat16)
        beside(i)


def updated(buf_in, hid, w_out, buf_out):
    cols = buf_in.shape[2]
    h = hid[...]
    for r in range(0, w_out.shape[0], STEP):
        t = jnp.dot(w_out[r : r + STEP, :], h, preferred_element_type=jnp.float32)
        for j in range(GROUP):
            old = buf_in[j, r : r + STEP, :].astype(jnp.float32)
            buf_out[j, r : r + STEP, :] = (old + t[:, j * cols : (j + 1) * cols]).astype(jnp.bfloat16)


def arrivals_of(hbm, row_of, vmem, sem, g, b):
    return [
        pltpu.make_async_copy(hbm.at[row_of(g * GROUP + j)], vmem.at[b, j], sem.at[b, j])
        for j in range(GROUP)
    ]


def departures(vmem, hbm, row_of, sem, g, b):
    return [
        pltpu.make_async_copy(vmem.at[b, j], hbm.at[row_of(g * GROUP + j)], sem.at[b, j])
        for j in range(GROUP)
    ]


def start(copies):
    for c in copies:
        c.start()


def wait(copies):
    for c in copies:
        c.wait()


def order_kernel(
    nwide, nnarrow, move, table_hbm, owner_hbm, slot_hbm, weight_hbm, order, meta_hbm,
    table, owner, slot, weight, meta, sem,
):
    blocks = owner.shape[0]
    stay = blocks - move
    pairs = [(table_hbm, table), (owner_hbm, owner), (slot_hbm, slot), (weight_hbm, weight)]
    loads = [pltpu.make_async_copy(src, dst, sem.at[i]) for i, (src, dst) in enumerate(pairs)]
    start(loads)
    me = lax.axis_index("wide")
    base = (me * nnarrow + lax.axis_index("narrow")) * blocks
    loads[0].wait()

    def look(s, counts):
        kept, gone = counts
        dest = lax.div(table[base + s], nnarrow * blocks)
        leaves = dest != me
        order[jnp.where(leaves, stay + gone, kept)] = s
        order[blocks + s] = dest
        order[2 * blocks + s] = lax.rem(2 * me - dest + nwide, nwide)
        step = leaves.astype(jnp.int32)
        return kept + 1 - step, gone + step

    lax.fori_loop(0, blocks, look, (jnp.int32(0), jnp.int32(0)))
    wait(loads[1:])
    meta[...] = jnp.zeros_like(meta)
    for k in range(move):
        s = order[stay + k]
        source = order[2 * blocks + s]
        cell = owner[pl.ds(s, 1), :] * OCN_DEV + slot[pl.ds(s, 1), :]
        meta[source, 0:1, :] = cell.astype(jnp.float32)
        meta[source, 1:2, :] = weight[pl.ds(s, 1), :]
    save = pltpu.make_async_copy(meta, meta_hbm, sem.at[len(pairs)])
    save.start()
    save.wait()


def row_parts(src, dst, sem):
    parts = []
    for i, r in enumerate(range(0, src.shape[0], STEP)):
        rows = pl.ds(r, STEP)
        parts.append(pltpu.make_async_copy(src.at[rows], dst.at[rows], sem.at[i]))
    return parts


def leaving_kernel(
    order, state, w_in_hbm, w_out_hbm, w_flux_hbm, out, flux,
    w_in, w_out, w_flux, buf_in, buf_out, hid, sem_w, sem_f, sem_in, sem_out,
):
    blocks, _, cols = state.shape
    move = flux.shape[0]
    stay = blocks - move

    def slot_of(k):
        return order[stay + k]

    def row_of(k):
        return order[blocks + order[stay + k]]

    groups = move // GROUP
    load_in = row_parts(w_in_hbm, w_in, sem_w.at[0])
    load_out = row_parts(w_out_hbm, w_out, sem_w.at[1])
    load_flux = pltpu.make_async_copy(w_flux_hbm, w_flux, sem_f)
    start(arrivals_of(state, slot_of, buf_in, sem_in, 0, 0))
    start(load_in)
    load_flux.start()
    for g in range(groups):
        b = g % 2
        wait(arrivals_of(state, slot_of, buf_in, sem_in, g, b))
        if g == 0:
            wait(load_in)
            start(load_out)
        if g + 1 < groups:
            start(arrivals_of(state, slot_of, buf_in, sem_in, g + 1, 1 - b))
        if g >= 2:
            wait(departures(buf_out, out, row_of, sem_out, g - 2, b))
        hidden_of(side_by_side(buf_in.at[b]), w_in, hid)
        if g == 0:
            wait(load_out)
        updated(buf_in.at[b], hid, w_out, buf_out.at[b])
        start(departures(buf_out, out, row_of, sem_out, g, b))
        if g == 0:
            load_flux.wait()
        f = jnp.dot(w_flux[...], hid[...], preferred_element_type=jnp.float32)
        for j in range(GROUP):
            flux[g * GROUP + j] = f[:, j * cols : (j + 1) * cols]
    for g in range(max(groups - 2, 0), groups):
        wait(departures(buf_out, out, row_of, sem_out, g, g % 2))


def staying_kernel(
    devices, nnarrow,
    order, state, w_in_hbm, w_out_hbm, w_flux_hbm, flux_away_hbm, meta_hbm, owner_hbm, slot_hbm, weight_hbm,
    hidden, kept, w_out, keep, send,
    w_in, w_flux, flux_away, meta, owner, slot, weight, cells, areas, lows, flux, left, right, total,
    sem_w, sem_s, sem_kept,
):
    groups, _, _, cols = kept.shape
    stay = groups * GROUP
    move = flux_away.shape[0]
    blocks = stay + move
    device = lax.axis_index("wide") * nnarrow + lax.axis_index("narrow")

    def arrivals(g):
        return arrivals_of(state, lambda k: order[k], kept, sem_kept, g, g)

    load_in = row_parts(w_in_hbm, w_in, sem_w.at[0])
    load_out = row_parts(w_out_hbm, w_out, sem_w.at[1])
    pairs = [
        (w_flux_hbm, w_flux), (owner_hbm, owner), (slot_hbm, slot), (weight_hbm, weight),
        (flux_away_hbm, flux_away), (meta_hbm, meta),
    ]
    small = [pltpu.make_async_copy(src, dst, sem_s.at[i]) for i, (src, dst) in enumerate(pairs)]
    start(arrivals(0))
    start(load_in)
    start(small)

    def tables():
        for c in range(blocks):
            here = pl.ds(order[c], 1)
            if c < stay:
                cells[c : c + 1, :] = (owner[here, :] * OCN_DEV + slot[here, :]).astype(jnp.float32)
                areas[c : c + 1, :] = weight[here, :]
            else:
                dest = order[blocks + order[c]]
                cells[c : c + 1, :] = meta[dest, 0:1, :]
                areas[c : c + 1, :] = meta[dest, 1:2, :]
        high, low = spread(devices, device, cells[...].astype(jnp.int32))
        cells[...] = high.astype(jnp.float32)
        lows[...] = low.astype(jnp.float32).T

    def factors(c, at, f):
        if isinstance(c, int):
            row, low = slice(c, c + 1), lows[:, c : c + 1]
        else:
            row = pl.ds(c, 1)
            lane = lax.broadcasted_iota(jnp.int32, (cols, blocks), 1)
            low = jnp.sum(jnp.where(lane == c, lows[...], 0.0), axis=1, keepdims=True)
        fill(at, devices * OCN_DEV // LANES, f, areas[row, :], cells[row, :], low, left, right)

    def one_hot(g, j):
        factors(g * GROUP + j, j * cols, flux[j])

    def work(g, beside):
        hidden_of(side_by_side(kept.at[g]), w_in, hidden.at[g], beside)
        f = jnp.dot(w_flux[...], hidden[g], preferred_element_type=jnp.float32)
        for j in range(GROUP):
            flux[j] = f[:, j * cols : (j + 1) * cols]

    wait(arrivals(0))
    wait(load_in)
    if groups > 1:
        start(arrivals(1))
    wait(small)
    tables()
    work(0, lambda i: None)

    def later(g):
        wait(arrivals(g))
        work(g, lambda i: one_hot(g - 1, i) if i < GROUP else None)

    if devices <= 32:
        for g in range(1, groups):
            if g + 1 < groups:
                start(arrivals(g + 1))
            else:
                start(load_out)
            later(g)
            add_product(total, left, right, g == 1)
    else:
        total[...] = jnp.zeros_like(total)

        @pl.loop(1, groups)
        def _(g):
            @pl.when(g + 1 < groups)
            def _():
                start(arrivals(g + 1))

            @pl.when(g + 1 == groups)
            def _():
                start(load_out)

            later(g)
            add_product(total, left, right, False)

    for j in range(GROUP):
        one_hot(groups - 1, j)
    add_product(total, left, right, False)
    for g in range(move // GROUP):
        for j in range(GROUP):
            k = g * GROUP + j
            factors(stay + k, j * cols, flux_away[k])
        add_product(total, left, right, False)
    half = total.shape[0] // 2
    keep[...] = total[:half, :]
    send[...] = total[half:, :].astype(jnp.bfloat16)
    wait(load_out)


def update_kernel(first, last, order, kept, hidden, w_out, *rest):
    out, buf_out, sem_out = rest[-3:]

    def slot_of(k):
        return order[k]

    @pl.loop(first, last)
    def _(g):
        updated(kept.at[g], hidden.at[g], w_out, buf_out.at[g - first])
        start(departures(buf_out, out, slot_of, sem_out, g, g - first))

    for g in range(first, last):
        wait(departures(buf_out, out, slot_of, sem_out, g, g - first))


def spread(devices, device, cell):
    bits = devices.bit_length() - 1
    apart = (cell // OCN_DEV) ^ device
    far = jnp.zeros_like(apart)
    for i in range(bits):
        far = far | (((apart >> i) & 1) << (bits - 1 - i))
    return far * (OCN_DEV // LANES) + cell % OCN_DEV // LANES, cell % LANES


def fill(at, highs, f, area, high, low, left, right):
    nflux, cols = f.shape
    bf16 = jnp.bfloat16
    f = (f * area).astype(bf16)
    high = jnp.broadcast_to(high, (nflux, cols)).astype(bf16)
    low = jnp.broadcast_to(low, (cols, LANES)).astype(bf16)
    lanes = lax.broadcasted_iota(jnp.int32, (cols, LANES), 1).astype(jnp.float32).astype(bf16)
    one, zero = jnp.ones((), bf16), jnp.zeros((), bf16)
    right[at : at + cols, :] = jnp.where(low == lanes, one, zero)
    for h in range(highs):
        left[h * nflux : (h + 1) * nflux, at : at + cols] = jnp.where(
            high == jnp.asarray(h, bf16), f, zero
        )


def add_product(total, left, right, first):
    h = right[...]
    for r in range(0, total.shape[0], CHUNK):
        p = jnp.dot(left[r : r + CHUNK, :], h, preferred_element_type=jnp.float32)
        total[r : r + CHUNK, :] = p if first else total[r : r + CHUNK, :] + p


def halve_kernel(mine, came, keep, *sends):
    rows = keep.shape[0]
    keep[...] = mine[:rows, :] + came[:rows, :].astype(jnp.float32)
    for i, send in enumerate(sends):
        at = pl.ds((i + 1) * rows, rows)
        send[...] = (mine[at, :] + came[at, :].astype(jnp.float32)).astype(jnp.bfloat16)


def place_kernel(move, order, arrived, _, out, sem):
    blocks = out.shape[0]
    stay = blocks - move
    copies = []
    for k in range(move):
        s = order[stay + k]
        copies.append(
            pltpu.make_async_copy(arrived.at[order[2 * blocks + s]], out.at[s], sem.at[k])
        )
    start(copies)
    wait(copies)


def last_kernel(mine, *rest):
    came, ocean = rest[:-2], rest[-1]
    nflux = ocean.shape[0]
    for h in range(OCN_DEV // LANES):
        rows = slice(h * nflux, (h + 1) * nflux)
        part = mine[rows, :]
        for c in came:
            part = part + c[rows, :].astype(jnp.float32)
        ocean[:, h * LANES : (h + 1) * LANES] = part


SMEM = pl.BlockSpec(memory_space=pltpu.SMEM)
VMEM = pl.BlockSpec(memory_space=pltpu.VMEM)
HBM = pl.BlockSpec(memory_space=pltpu.HBM)
ANY = pl.BlockSpec(memory_space=pl.ANY)


def per_device(state, group_of, w_in, w_out, w_flux, owner, ocean_slot, remap_weight):
    nwide = lax.axis_size("wide")
    nnarrow = lax.axis_size("narrow")
    blocks, depth, cols = state.shape
    inner = w_in.shape[0]
    nflux = w_flux.shape[0]
    devices = nwide * nnarrow
    move = nwide // 2
    stay = blocks - move
    bf16, f32, i32 = jnp.bfloat16, jnp.float32, jnp.int32
    shape = jax.ShapeDtypeStruct
    dma = pltpu.SemaphoreType.DMA
    side = GROUP * cols
    owner = owner[:, 0].reshape(blocks, cols)
    slot = ocean_slot.reshape(blocks, cols)
    weight = remap_weight.reshape(blocks, cols)
    params = pltpu.CompilerParams(vmem_limit_bytes=20 * MIB)
    in_hbm = functools.partial(pltpu.with_memory_space_constraint, memory_space=pltpu.HBM)
    in_vmem = functools.partial(pltpu.with_memory_space_constraint, memory_space=pltpu.VMEM)

    def cost(n, products):
        return pl.CostEstimate(
            flops=2 * n * cols * inner * depth * products,
            bytes_accessed=4 * n * depth * cols + 2 * inner * depth * products,
            transcendentals=n * cols * inner,
        )

    def swap(x, axis, bit):
        return lax.ppermute(x, axis, [(i, i ^ bit) for i in range(lax.axis_size(axis))])

    with jax.named_scope("order_of_blocks"):
        order, meta = pl.pallas_call(
            functools.partial(order_kernel, nwide, nnarrow, move),
            out_shape=(shape((3 * blocks,), i32), pltpu.HBM((nwide, 8, cols), f32)),
            in_specs=[HBM] * 4,
            out_specs=(SMEM, HBM),
            scratch_shapes=[
                pltpu.SMEM(group_of.shape, i32),
                pltpu.VMEM((blocks, cols), i32),
                pltpu.VMEM((blocks, cols), i32),
                pltpu.VMEM((blocks, cols), f32),
                pltpu.VMEM((nwide, 8, cols), f32),
                dma((5,)),
            ],
            compiler_params=params,
        )(in_hbm(group_of), in_hbm(owner), in_hbm(slot), in_hbm(weight))
    meta = lax.all_to_all(meta, "wide", split_axis=0, concat_axis=0, tiled=True)

    groups = stay // GROUP
    parts = max(inner, depth) // STEP
    with jax.named_scope("leaving_blocks"):
        outgoing, flux_away = pl.pallas_call(
            leaving_kernel,
            out_shape=(pltpu.HBM((nwide, depth, cols), bf16), pltpu.HBM((move, nflux, cols), f32)),
            in_specs=[SMEM, HBM, HBM, HBM, HBM],
            out_specs=(HBM, VMEM),
            scratch_shapes=[
                pltpu.VMEM((inner, depth), bf16),
                pltpu.VMEM((depth, inner), bf16),
                pltpu.VMEM((nflux, inner), bf16),
                pltpu.VMEM((2, GROUP, depth, cols), bf16),
                pltpu.VMEM((2, GROUP, depth, cols), bf16),
                pltpu.VMEM((inner, side), bf16),
                dma((2, parts)),
                dma,
                dma((2, GROUP)),
                dma((2, GROUP)),
            ],
            compiler_params=params,
            cost_estimate=cost(move, 2),
        )(order, in_hbm(state), in_hbm(w_in), in_hbm(w_out), in_hbm(w_flux))
    outgoing, meta = lax.optimization_barrier((outgoing, meta))
    arrived = lax.all_to_all(outgoing, "wide", split_axis=0, concat_axis=0, tiled=True)

    rows = devices * nflux * OCN_DEV // LANES
    with jax.named_scope("staying_blocks_and_cell_sums"):
        hidden, kept, w_out, keep, send = pl.pallas_call(
            functools.partial(staying_kernel, devices, nnarrow),
            out_shape=(
                pltpu.VMEM((groups, inner, side), bf16),
                pltpu.VMEM((groups, GROUP, depth, cols), bf16),
                pltpu.VMEM(w_out.shape, bf16),
                shape((rows // 2, LANES), f32),
                shape((rows // 2, LANES), bf16),
            ),
            in_specs=[SMEM] + [HBM] * 9,
            out_specs=(VMEM,) * 5,
            scratch_shapes=[
                pltpu.VMEM((inner, depth), bf16),
                pltpu.VMEM((nflux, inner), bf16),
                pltpu.VMEM((move, nflux, cols), f32),
                pltpu.VMEM((nwide, 8, cols), f32),
                pltpu.VMEM((blocks, cols), i32),
                pltpu.VMEM((blocks, cols), i32),
                pltpu.VMEM((blocks, cols), f32),
                pltpu.VMEM((blocks, cols), f32),
                pltpu.VMEM((blocks, cols), f32),
                pltpu.VMEM((cols, blocks), f32),
                pltpu.VMEM((GROUP, nflux, cols), f32),
                pltpu.VMEM((rows, side), bf16),
                pltpu.VMEM((side, LANES), bf16),
                pltpu.VMEM((rows, LANES), f32),
                dma((2, parts)),
                dma((6,)),
                dma((groups, GROUP)),
            ],
            compiler_params=pltpu.CompilerParams(vmem_limit_bytes=20 * MIB + 14 * rows * LANES),
            cost_estimate=pl.CostEstimate(
                flops=2 * cols * (stay * inner * depth + rows * LANES * blocks),
                bytes_accessed=2 * stay * depth * cols + 4 * inner * depth,
                transcendentals=stay * cols * inner,
            ),
        )(
            order,
            *map(in_hbm, (state, w_in, w_out, w_flux, flux_away, meta, owner, slot, weight)),
        )

    partial = None
    done = 0

    def update(upto, partial, after):
        begun = () if partial is None else (partial,)
        return pl.pallas_call(
            functools.partial(update_kernel, done, upto),
            out_shape=shape(state.shape, bf16),
            in_specs=[SMEM, VMEM, VMEM, VMEM, ANY] + [ANY] * len(begun),
            out_specs=ANY,
            scratch_shapes=[
                pltpu.VMEM((upto - done, GROUP, depth, cols), bf16),
                dma((upto - done, GROUP)),
            ],
            input_output_aliases={5: 0} if begun else {},
            compiler_params=params,
            cost_estimate=cost((upto - done) * GROUP, 1),
        )(order, in_vmem(kept), in_vmem(hidden), in_vmem(w_out), after, *begun)

    bits = [("narrow", 1 << i) for i in range(nnarrow.bit_length() - 1)]
    bits += [("wide", 1 << i) for i in range(nwide.bit_length() - 3)]
    own = nflux * OCN_DEV // LANES
    rows //= 2
    sends = (send,)
    with jax.named_scope("ocean_sums"):
        for i, (axis, bit) in enumerate(bits):
            came = swap(sends[0], axis, bit)
            if i > 0:
                upto = min(groups, done + -(-groups // len(bits)))
                if upto > done:
                    with jax.named_scope("update_of_staying_blocks"):
                        partial = update(upto, partial, keep)
                    done = upto
            quarters = i == len(bits) - 1
            rows = own if quarters else rows // 2
            count = 3 if quarters else 1
            keep, *sends = pl.pallas_call(
                halve_kernel,
                out_shape=(shape((rows, LANES), f32),) + (shape((rows, LANES), bf16),) * count,
                in_specs=[VMEM, VMEM],
                out_specs=(VMEM,) * (1 + count),
                compiler_params=params,
            )(keep, came)
        came = [swap(x, "wide", d * nwide // 4) for x, d in zip(sends, (2, 1, 3))]
        with jax.named_scope("update_of_staying_blocks"):
            partial = update(groups, partial, keep)

    with jax.named_scope("arrived_blocks"):
        new_state = pl.pallas_call(
            functools.partial(place_kernel, move),
            out_shape=shape(state.shape, bf16),
            in_specs=[SMEM, VMEM, ANY],
            out_specs=ANY,
            scratch_shapes=[dma((move,))],
            input_output_aliases={2: 0},
            compiler_params=params,
        )(order, arrived, partial)
    with jax.named_scope("last_sums"):
        ocean = pl.pallas_call(
            last_kernel,
            out_shape=shape((nflux, OCN_DEV), f32),
            in_specs=[VMEM] * 4 + [HBM],
            out_specs=VMEM,
            compiler_params=params,
        )(keep, *came, in_hbm(new_state))
    return (new_state, ocean)


def solution(mesh):
    in_specs = (
        P(("wide", "narrow"), None, None),
        P(),
        P(),
        P(),
        P(),
        P(("wide", "narrow"), None),
        P(("wide", "narrow")),
        P(("wide", "narrow")),
    )
    out_specs = (P(("wide", "narrow"), None, None), P(None, ("wide", "narrow")))
    return jax.shard_map(
        per_device, mesh=mesh, in_specs=in_specs, out_specs=out_specs, check_vma=False
    )
```

```python
import functools

import jax
import jax.numpy as jnp
from jax import lax
from jax.experimental import pallas as pl
from jax.experimental.pallas import tpu as pltpu
from jax.sharding import PartitionSpec as P

OCN_DEV = 512
LANES = 256
GROUP = 4
STEP = 256
CHUNK = 512
MIB = 1024 * 1024


def silu(v):
    u = 0.5 * v
    return u + u * jnp.tanh(u)


def side_by_side(blocks):
    return jnp.concatenate([blocks[j] for j in range(GROUP)], axis=1)


def hidden_of(x, w_in, hid, beside=lambda i: None):
    for i, r in enumerate(range(0, w_in.shape[0], STEP)):
        v = jnp.dot(w_in[r : r + STEP, :], x, preferred_element_type=jnp.float32)
        hid[r : r + STEP, :] = silu(v).astype(jnp.bfloat16)
        beside(i)


def updated(buf_in, hid, w_out, buf_out):
    cols = buf_in.shape[2]
    h = hid[...]
    for r in range(0, w_out.shape[0], STEP):
        t = jnp.dot(w_out[r : r + STEP, :], h, preferred_element_type=jnp.float32)
        for j in range(GROUP):
            old = buf_in[j, r : r + STEP, :].astype(jnp.float32)
            buf_out[j, r : r + STEP, :] = (old + t[:, j * cols : (j + 1) * cols]).astype(jnp.bfloat16)


def arrivals_of(hbm, row_of, vmem, sem, g, b):
    return [
        pltpu.make_async_copy(hbm.at[row_of(g * GROUP + j)], vmem.at[b, j], sem.at[b, j])
        for j in range(GROUP)
    ]


def departures(vmem, hbm, row_of, sem, g, b):
    return [
        pltpu.make_async_copy(vmem.at[b, j], hbm.at[row_of(g * GROUP + j)], sem.at[b, j])
        for j in range(GROUP)
    ]


def start(copies):
    for c in copies:
        c.start()


def wait(copies):
    for c in copies:
        c.wait()


def order_kernel(
    nwide, nnarrow, move, table_hbm, owner_hbm, slot_hbm, weight_hbm, order, meta_hbm,
    table, owner, slot, weight, meta, sem,
):
    blocks = owner.shape[0]
    stay = blocks - move
    pairs = [(table_hbm, table), (owner_hbm, owner), (slot_hbm, slot), (weight_hbm, weight)]
    loads = [pltpu.make_async_copy(src, dst, sem.at[i]) for i, (src, dst) in enumerate(pairs)]
    start(loads)
    me = lax.axis_index("wide")
    base = (me * nnarrow + lax.axis_index("narrow")) * blocks
    loads[0].wait()

    def look(s, counts):
        kept, gone = counts
        dest = lax.div(table[base + s], nnarrow * blocks)
        leaves = dest != me
        order[jnp.where(leaves, stay + gone, kept)] = s
        order[blocks + s] = dest
        order[2 * blocks + s] = lax.rem(2 * me - dest + nwide, nwide)
        step = leaves.astype(jnp.int32)
        return kept + 1 - step, gone + step

    lax.fori_loop(0, blocks, look, (jnp.int32(0), jnp.int32(0)), unroll=True)
    wait(loads[1:])
    meta[...] = jnp.zeros_like(meta)
    for k in range(move):
        s = order[stay + k]
        source = order[2 * blocks + s]
        cell = owner[pl.ds(s, 1), :] * OCN_DEV + slot[pl.ds(s, 1), :]
        meta[source, 0:1, :] = cell.astype(jnp.float32)
        meta[source, 1:2, :] = weight[pl.ds(s, 1), :]
    save = pltpu.make_async_copy(meta, meta_hbm, sem.at[len(pairs)])
    save.start()
    save.wait()


def row_parts(src, dst, sem):
    parts = []
    for i, r in enumerate(range(0, src.shape[0], STEP)):
        rows = pl.ds(r, STEP)
        parts.append(pltpu.make_async_copy(src.at[rows], dst.at[rows], sem.at[i]))
    return parts


def leaving_kernel(
    order, state, w_in_hbm, w_out_hbm, w_flux_hbm, out, flux_hbm,
    w_in, w_out, w_flux, flux, buf_in, buf_out, hid, sem_w, sem_f, sem_in, sem_out,
):
    blocks, _, cols = state.shape
    move = flux.shape[0]
    stay = blocks - move

    def slot_of(k):
        return order[stay + k]

    def row_of(k):
        return order[blocks + order[stay + k]]

    groups = move // GROUP
    load_in = row_parts(w_in_hbm, w_in, sem_w.at[0])
    load_out = row_parts(w_out_hbm, w_out, sem_w.at[1])
    load_flux = pltpu.make_async_copy(w_flux_hbm, w_flux, sem_f.at[0])
    start(arrivals_of(state, slot_of, buf_in, sem_in, 0, 0))
    start(load_in)
    load_flux.start()
    for g in range(groups):
        b = g % 2
        wait(arrivals_of(state, slot_of, buf_in, sem_in, g, b))
        if g == 0:
            wait(load_in)
            start(load_out)
        if g + 1 < groups:
            start(arrivals_of(state, slot_of, buf_in, sem_in, g + 1, 1 - b))
        if g >= 2:
            wait(departures(buf_out, out, row_of, sem_out, g - 2, b))
        hidden_of(side_by_side(buf_in.at[b]), w_in, hid)
        if g == 0:
            wait(load_out)
        updated(buf_in.at[b], hid, w_out, buf_out.at[b])
        start(departures(buf_out, out, row_of, sem_out, g, b))
        if g == 0:
            load_flux.wait()
        f = jnp.dot(w_flux[...], hid[...], preferred_element_type=jnp.float32)
        for j in range(GROUP):
            flux[g * GROUP + j] = f[:, j * cols : (j + 1) * cols]
    save = pltpu.make_async_copy(flux, flux_hbm, sem_f.at[1])
    save.start()
    for g in range(max(groups - 2, 0), groups):
        wait(departures(buf_out, out, row_of, sem_out, g, g % 2))
    save.wait()


def staying_kernel(
    devices, nnarrow,
    order, state, w_in_hbm, w_out_hbm, w_flux_hbm, flux_away_hbm, meta_hbm, owner_hbm, slot_hbm, weight_hbm,
    hidden, kept, w_out, keep, send,
    w_in, w_flux, flux_away, meta, owner, slot, weight, cells, areas, lows, flux, left, right, total,
    sem_w, sem_s, sem_kept,
):
    groups, _, _, cols = kept.shape
    stay = groups * GROUP
    move = flux_away.shape[0]
    blocks = stay + move
    device = lax.axis_index("wide") * nnarrow + lax.axis_index("narrow")

    def arrivals(g):
        return arrivals_of(state, lambda k: order[k], kept, sem_kept, g, g)

    load_in = row_parts(w_in_hbm, w_in, sem_w.at[0])
    load_out = row_parts(w_out_hbm, w_out, sem_w.at[1])
    pairs = [
        (w_flux_hbm, w_flux), (owner_hbm, owner), (slot_hbm, slot), (weight_hbm, weight),
        (flux_away_hbm, flux_away), (meta_hbm, meta),
    ]
    small = [pltpu.make_async_copy(src, dst, sem_s.at[i]) for i, (src, dst) in enumerate(pairs)]
    start(arrivals(0))
    start(load_in)
    start(small)

    def tables():
        for c in range(blocks):
            here = pl.ds(order[c], 1)
            if c < stay:
                cells[c : c + 1, :] = (owner[here, :] * OCN_DEV + slot[here, :]).astype(jnp.float32)
                areas[c : c + 1, :] = weight[here, :]
            else:
                dest = order[blocks + order[c]]
                cells[c : c + 1, :] = meta[dest, 0:1, :]
                areas[c : c + 1, :] = meta[dest, 1:2, :]
        high, low = spread(devices, device, cells[...].astype(jnp.int32))
        cells[...] = high.astype(jnp.float32)
        lows[...] = low.astype(jnp.float32).T

    def factors(c, at, f):
        if isinstance(c, int):
            row, low = slice(c, c + 1), lows[:, c : c + 1]
        else:
            row = pl.ds(c, 1)
            lane = lax.broadcasted_iota(jnp.int32, (cols, blocks), 1)
            low = jnp.sum(jnp.where(lane == c, lows[...], 0.0), axis=1, keepdims=True)
        fill(at, devices * OCN_DEV // LANES, f, areas[row, :], cells[row, :], low, left, right)

    def one_hot(g, j):
        factors(g * GROUP + j, j * cols, flux[j])

    def work(g, beside):
        hidden_of(side_by_side(kept.at[g]), w_in, hidden.at[g], beside)
        f = jnp.dot(w_flux[...], hidden[g], preferred_element_type=jnp.float32)
        for j in range(GROUP):
            flux[j] = f[:, j * cols : (j + 1) * cols]

    wait(arrivals(0))
    wait(load_in)
    if groups > 1:
        start(arrivals(1))
    wait(small)
    tables()
    work(0, lambda i: None)

    def later(g):
        wait(arrivals(g))
        work(g, lambda i: one_hot(g - 1, i) if i < GROUP else None)

    if devices <= 32:
        for g in range(1, groups):
            if g + 1 < groups:
                start(arrivals(g + 1))
            else:
                start(load_out)
            later(g)
            add_product(total, left, right, g == 1)
    else:
        total[...] = jnp.zeros_like(total)

        @pl.loop(1, groups)
        def _(g):
            @pl.when(g + 1 < groups)
            def _():
                start(arrivals(g + 1))

            @pl.when(g + 1 == groups)
            def _():
                start(load_out)

            later(g)
            add_product(total, left, right, False)

    for j in range(GROUP):
        one_hot(groups - 1, j)
    add_product(total, left, right, False)
    for g in range(move // GROUP):
        for j in range(GROUP):
            k = g * GROUP + j
            factors(stay + k, j * cols, flux_away[k])
        add_product(total, left, right, False)
    half = total.shape[0] // 2
    keep[...] = total[:half, :]
    send[...] = total[half:, :].astype(jnp.bfloat16)
    wait(load_out)


def update_kernel(first, last, order, kept, hidden, w_out, *rest):
    out, buf_out, sem_out = rest[-3:]

    def slot_of(k):
        return order[k]

    @pl.loop(first, last)
    def _(g):
        updated(kept.at[g], hidden.at[g], w_out, buf_out.at[g - first])
        start(departures(buf_out, out, slot_of, sem_out, g, g - first))

    for g in range(first, last):
        wait(departures(buf_out, out, slot_of, sem_out, g, g - first))


def spread(devices, device, cell):
    bits = devices.bit_length() - 1
    apart = (cell // OCN_DEV) ^ device
    far = jnp.zeros_like(apart)
    for i in range(bits):
        far = far | (((apart >> i) & 1) << (bits - 1 - i))
    return far * (OCN_DEV // LANES) + cell % OCN_DEV // LANES, cell % LANES


def fill(at, highs, f, area, high, low, left, right):
    nflux, cols = f.shape
    bf16 = jnp.bfloat16
    f = (f * area).astype(bf16)
    high = jnp.broadcast_to(high, (nflux, cols)).astype(bf16)
    low = jnp.broadcast_to(low, (cols, LANES)).astype(bf16)
    lanes = lax.broadcasted_iota(jnp.int32, (cols, LANES), 1).astype(jnp.float32).astype(bf16)
    one, zero = jnp.ones((), bf16), jnp.zeros((), bf16)
    right[at : at + cols, :] = jnp.where(low == lanes, one, zero)
    for h in range(highs):
        left[h * nflux : (h + 1) * nflux, at : at + cols] = jnp.where(
            high == jnp.asarray(h, bf16), f, zero
        )


def add_product(total, left, right, first):
    h = right[...]
    for r in range(0, total.shape[0], CHUNK):
        p = jnp.dot(left[r : r + CHUNK, :], h, preferred_element_type=jnp.float32)
        total[r : r + CHUNK, :] = p if first else total[r : r + CHUNK, :] + p


def halve_kernel(mine, came, keep, *sends):
    rows = keep.shape[0]
    keep[...] = mine[:rows, :] + came[:rows, :].astype(jnp.float32)
    for i, send in enumerate(sends):
        at = pl.ds((i + 1) * rows, rows)
        send[...] = (mine[at, :] + came[at, :].astype(jnp.float32)).astype(jnp.bfloat16)


def place_kernel(move, order, arrived, _, out, sem):
    blocks = out.shape[0]
    stay = blocks - move
    copies = []
    for k in range(move):
        s = order[stay + k]
        copies.append(
            pltpu.make_async_copy(arrived.at[order[2 * blocks + s]], out.at[s], sem.at[k])
        )
    start(copies)
    wait(copies)


def last_kernel(mine, *rest):
    came, ocean = rest[:-2], rest[-1]
    nflux = ocean.shape[0]
    for h in range(OCN_DEV // LANES):
        rows = slice(h * nflux, (h + 1) * nflux)
        part = mine[rows, :]
        for c in came:
            part = part + c[rows, :].astype(jnp.float32)
        ocean[:, h * LANES : (h + 1) * LANES] = part


SMEM = pl.BlockSpec(memory_space=pltpu.SMEM)
VMEM = pl.BlockSpec(memory_space=pltpu.VMEM)
HBM = pl.BlockSpec(memory_space=pltpu.HBM)
ANY = pl.BlockSpec(memory_space=pl.ANY)


def per_device(state, group_of, w_in, w_out, w_flux, owner, ocean_slot, remap_weight):
    nwide = lax.axis_size("wide")
    nnarrow = lax.axis_size("narrow")
    blocks, depth, cols = state.shape
    inner = w_in.shape[0]
    nflux = w_flux.shape[0]
    devices = nwide * nnarrow
    move = nwide // 2
    stay = blocks - move
    bf16, f32, i32 = jnp.bfloat16, jnp.float32, jnp.int32
    shape = jax.ShapeDtypeStruct
    dma = pltpu.SemaphoreType.DMA
    side = GROUP * cols
    owner = owner[:, 0].reshape(blocks, cols)
    slot = ocean_slot.reshape(blocks, cols)
    weight = remap_weight.reshape(blocks, cols)
    params = pltpu.CompilerParams(vmem_limit_bytes=20 * MIB)
    in_hbm = functools.partial(pltpu.with_memory_space_constraint, memory_space=pltpu.HBM)
    in_vmem = functools.partial(pltpu.with_memory_space_constraint, memory_space=pltpu.VMEM)

    def cost(n, products):
        return pl.CostEstimate(
            flops=2 * n * cols * inner * depth * products,
            bytes_accessed=4 * n * depth * cols + 2 * inner * depth * products,
            transcendentals=n * cols * inner,
        )

    def swap(x, axis, bit):
        return lax.ppermute(x, axis, [(i, i ^ bit) for i in range(lax.axis_size(axis))])

    with jax.named_scope("order_of_blocks"):
        order, meta = pl.pallas_call(
            functools.partial(order_kernel, nwide, nnarrow, move),
            out_shape=(shape((3 * blocks,), i32), pltpu.HBM((nwide, 8, cols), f32)),
            in_specs=[HBM] * 4,
            out_specs=(SMEM, HBM),
            scratch_shapes=[
                pltpu.SMEM(group_of.shape, i32),
                pltpu.VMEM((blocks, cols), i32),
                pltpu.VMEM((blocks, cols), i32),
                pltpu.VMEM((blocks, cols), f32),
                pltpu.VMEM((nwide, 8, cols), f32),
                dma((5,)),
            ],
            compiler_params=params,
        )(in_hbm(group_of), in_hbm(owner), in_hbm(slot), in_hbm(weight))
    meta = lax.all_to_all(meta, "wide", split_axis=0, concat_axis=0, tiled=True)

    groups = stay // GROUP
    parts = max(inner, depth) // STEP
    with jax.named_scope("leaving_blocks"):
        outgoing, flux_away = pl.pallas_call(
            leaving_kernel,
            out_shape=(pltpu.HBM((nwide, depth, cols), bf16), pltpu.HBM((move, nflux, cols), f32)),
            in_specs=[SMEM, HBM, HBM, HBM, HBM],
            out_specs=(HBM, HBM),
            scratch_shapes=[
                pltpu.VMEM((inner, depth), bf16),
                pltpu.VMEM((depth, inner), bf16),
                pltpu.VMEM((nflux, inner), bf16),
                pltpu.VMEM((move, nflux, cols), f32),
                pltpu.VMEM((2, GROUP, depth, cols), bf16),
                pltpu.VMEM((2, GROUP, depth, cols), bf16),
                pltpu.VMEM((inner, side), bf16),
                dma((2, parts)),
                dma((2,)),
                dma((2, GROUP)),
                dma((2, GROUP)),
            ],
            compiler_params=params,
            cost_estimate=cost(move, 2),
        )(order, in_hbm(state), in_hbm(w_in), in_hbm(w_out), in_hbm(w_flux))
    outgoing, meta = lax.optimization_barrier((outgoing, meta))
    arrived = lax.all_to_all(outgoing, "wide", split_axis=0, concat_axis=0, tiled=True)

    rows = devices * nflux * OCN_DEV // LANES
    with jax.named_scope("staying_blocks_and_cell_sums"):
        hidden, kept, w_out, keep, send = pl.pallas_call(
            functools.partial(staying_kernel, devices, nnarrow),
            out_shape=(
                pltpu.VMEM((groups, inner, side), bf16),
                pltpu.VMEM((groups, GROUP, depth, cols), bf16),
                pltpu.VMEM(w_out.shape, bf16),
                shape((rows // 2, LANES), f32),
                shape((rows // 2, LANES), bf16),
            ),
            in_specs=[SMEM] + [HBM] * 9,
            out_specs=(VMEM,) * 5,
            scratch_shapes=[
                pltpu.VMEM((inner, depth), bf16),
                pltpu.VMEM((nflux, inner), bf16),
                pltpu.VMEM((move, nflux, cols), f32),
                pltpu.VMEM((nwide, 8, cols), f32),
                pltpu.VMEM((blocks, cols), i32),
                pltpu.VMEM((blocks, cols), i32),
                pltpu.VMEM((blocks, cols), f32),
                pltpu.VMEM((blocks, cols), f32),
                pltpu.VMEM((blocks, cols), f32),
                pltpu.VMEM((cols, blocks), f32),
                pltpu.VMEM((GROUP, nflux, cols), f32),
                pltpu.VMEM((rows, side), bf16),
                pltpu.VMEM((side, LANES), bf16),
                pltpu.VMEM((rows, LANES), f32),
                dma((2, parts)),
                dma((6,)),
                dma((groups, GROUP)),
            ],
            compiler_params=pltpu.CompilerParams(vmem_limit_bytes=20 * MIB + 14 * rows * LANES),
            cost_estimate=pl.CostEstimate(
                flops=2 * cols * (stay * inner * depth + rows * LANES * blocks),
                bytes_accessed=2 * stay * depth * cols + 4 * inner * depth,
                transcendentals=stay * cols * inner,
            ),
        )(
            order,
            *map(in_hbm, (state, w_in, w_out, w_flux, flux_away, meta, owner, slot, weight)),
        )

    partial = None
    done = 0

    def update(upto, partial, after):
        begun = () if partial is None else (partial,)
        return pl.pallas_call(
            functools.partial(update_kernel, done, upto),
            out_shape=shape(state.shape, bf16),
            in_specs=[SMEM, VMEM, VMEM, VMEM, ANY] + [ANY] * len(begun),
            out_specs=ANY,
            scratch_shapes=[
                pltpu.VMEM((upto - done, GROUP, depth, cols), bf16),
                dma((upto - done, GROUP)),
            ],
            input_output_aliases={5: 0} if begun else {},
            compiler_params=params,
            cost_estimate=cost((upto - done) * GROUP, 1),
        )(order, in_vmem(kept), in_vmem(hidden), in_vmem(w_out), after, *begun)

    bits = [("narrow", 1 << i) for i in range(nnarrow.bit_length() - 1)]
    bits += [("wide", 1 << i) for i in range(nwide.bit_length() - 3)]
    own = nflux * OCN_DEV // LANES
    rows //= 2
    sends = (send,)
    with jax.named_scope("ocean_sums"):
        for i, (axis, bit) in enumerate(bits):
            came = swap(sends[0], axis, bit)
            if i > 0:
                upto = min(groups, done + -(-groups // len(bits)))
                if upto > done:
                    with jax.named_scope("update_of_staying_blocks"):
                        partial = update(upto, partial, keep)
                    done = upto
            quarters = i == len(bits) - 1
            rows = own if quarters else rows // 2
            count = 3 if quarters else 1
            keep, *sends = pl.pallas_call(
                halve_kernel,
                out_shape=(shape((rows, LANES), f32),) + (shape((rows, LANES), bf16),) * count,
                in_specs=[VMEM, VMEM],
                out_specs=(VMEM,) * (1 + count),
                compiler_params=params,
            )(keep, came)
        came = [swap(x, "wide", d * nwide // 4) for x, d in zip(sends, (2, 1, 3))]
        with jax.named_scope("update_of_staying_blocks"):
            partial = update(groups, partial, keep)

    with jax.named_scope("arrived_blocks"):
        new_state = pl.pallas_call(
            functools.partial(place_kernel, move),
            out_shape=shape(state.shape, bf16),
            in_specs=[SMEM, VMEM, ANY],
            out_specs=ANY,
            scratch_shapes=[dma((move,))],
            input_output_aliases={2: 0},
            compiler_params=params,
        )(order, arrived, partial)
    with jax.named_scope("last_sums"):
        ocean = pl.pallas_call(
            last_kernel,
            out_shape=shape((nflux, OCN_DEV), f32),
            in_specs=[VMEM] * 4 + [HBM],
            out_specs=VMEM,
            compiler_params=params,
        )(keep, *came, in_hbm(new_state))
    return (new_state, ocean)


def solution(mesh):
    in_specs = (
        P(("wide", "narrow"), None, None),
        P(),
        P(),
        P(),
        P(),
        P(("wide", "narrow"), None),
        P(("wide", "narrow")),
        P(("wide", "narrow")),
    )
    out_specs = (P(("wide", "narrow"), None, None), P(None, ("wide", "narrow")))
    return jax.shard_map(
        per_device, mesh=mesh, in_specs=in_specs, out_specs=out_specs, check_vma=False
    )
```

```python
import functools

import jax
import jax.numpy as jnp
from jax import lax
from jax.experimental import pallas as pl
from jax.experimental.pallas import tpu as pltpu
from jax.sharding import PartitionSpec as P

OCN_DEV = 512
LANES = 256
GROUP = 4
STEP = 256
CHUNK = 512
MIB = 1024 * 1024


def silu(v):
    u = 0.5 * v
    return u + u * jnp.tanh(u)


def side_by_side(blocks):
    return jnp.concatenate([blocks[j] for j in range(GROUP)], axis=1)


def hidden_of(x, w_in, hid, beside=lambda i: None):
    for i, r in enumerate(range(0, w_in.shape[0], STEP)):
        v = jnp.dot(w_in[r : r + STEP, :], x, preferred_element_type=jnp.float32)
        hid[r : r + STEP, :] = silu(v).astype(jnp.bfloat16)
        beside(i)


def updated(buf_in, hid, w_out, buf_out):
    cols = buf_in.shape[2]
    h = hid[...]
    for r in range(0, w_out.shape[0], STEP):
        t = jnp.dot(w_out[r : r + STEP, :], h, preferred_element_type=jnp.float32)
        for j in range(GROUP):
            old = buf_in[j, r : r + STEP, :].astype(jnp.float32)
            buf_out[j, r : r + STEP, :] = (old + t[:, j * cols : (j + 1) * cols]).astype(jnp.bfloat16)


def arrivals_of(hbm, row_of, vmem, sem, g, b):
    return [
        pltpu.make_async_copy(hbm.at[row_of(g * GROUP + j)], vmem.at[b, j], sem.at[b, j])
        for j in range(GROUP)
    ]


def departures(vmem, hbm, row_of, sem, g, b):
    return [
        pltpu.make_async_copy(vmem.at[b, j], hbm.at[row_of(g * GROUP + j)], sem.at[b, j])
        for j in range(GROUP)
    ]


def start(copies):
    for c in copies:
        c.start()


def wait(copies):
    for c in copies:
        c.wait()


def order_kernel(
    nwide, nnarrow, move, table_hbm, owner_hbm, slot_hbm, weight_hbm, order_hbm, meta_hbm,
    order, table, owner, slot, weight, meta, sem,
):
    blocks = owner.shape[0]
    stay = blocks - move
    pairs = [(table_hbm, table), (owner_hbm, owner), (slot_hbm, slot), (weight_hbm, weight)]
    loads = [pltpu.make_async_copy(src, dst, sem.at[i]) for i, (src, dst) in enumerate(pairs)]
    start(loads)
    me = lax.axis_index("wide")
    base = (me * nnarrow + lax.axis_index("narrow")) * blocks
    loads[0].wait()

    def look(s, counts):
        kept, gone = counts
        dest = lax.div(table[base + s], nnarrow * blocks)
        leaves = dest != me
        order[jnp.where(leaves, stay + gone, kept)] = s
        order[blocks + s] = dest
        order[2 * blocks + s] = lax.rem(2 * me - dest + nwide, nwide)
        step = leaves.astype(jnp.int32)
        return kept + 1 - step, gone + step

    lax.fori_loop(0, blocks, look, (jnp.int32(0), jnp.int32(0)), unroll=True)
    save_order = pltpu.make_async_copy(order, order_hbm, sem.at[len(pairs) + 1])
    save_order.start()
    wait(loads[1:])
    meta[...] = jnp.zeros_like(meta)
    for k in range(move):
        s = order[stay + k]
        source = order[2 * blocks + s]
        cell = owner[pl.ds(s, 1), :] * OCN_DEV + slot[pl.ds(s, 1), :]
        meta[source, 0:1, :] = cell.astype(jnp.float32)
        meta[source, 1:2, :] = weight[pl.ds(s, 1), :]
    save = pltpu.make_async_copy(meta, meta_hbm, sem.at[len(pairs)])
    save.start()
    save.wait()
    save_order.wait()


def row_parts(src, dst, sem):
    parts = []
    for i, r in enumerate(range(0, src.shape[0], STEP)):
        rows = pl.ds(r, STEP)
        parts.append(pltpu.make_async_copy(src.at[rows], dst.at[rows], sem.at[i]))
    return parts


def leaving_kernel(
    order_hbm, state, w_in_hbm, w_out_hbm, w_flux_hbm, out, flux_hbm,
    w_in, w_out, w_flux, flux, order, buf_in, buf_out, hid, sem_w, sem_f, sem_in, sem_out,
):
    blocks, _, cols = state.shape
    move = flux.shape[0]
    stay = blocks - move

    def slot_of(k):
        return order[stay + k]

    def row_of(k):
        return order[blocks + order[stay + k]]

    groups = move // GROUP
    load_in = row_parts(w_in_hbm, w_in, sem_w.at[0])
    load_out = row_parts(w_out_hbm, w_out, sem_w.at[1])
    load_flux = pltpu.make_async_copy(w_flux_hbm, w_flux, sem_f.at[0])
    load_order = pltpu.make_async_copy(order_hbm, order, sem_f.at[2])
    load_order.start()
    start(load_in)
    load_order.wait()
    start(arrivals_of(state, slot_of, buf_in, sem_in, 0, 0))
    load_flux.start()
    for g in range(groups):
        b = g % 2
        wait(arrivals_of(state, slot_of, buf_in, sem_in, g, b))
        if g == 0:
            wait(load_in)
            start(load_out)
        if g + 1 < groups:
            start(arrivals_of(state, slot_of, buf_in, sem_in, g + 1, 1 - b))
        if g >= 2:
            wait(departures(buf_out, out, row_of, sem_out, g - 2, b))
        hidden_of(side_by_side(buf_in.at[b]), w_in, hid)
        if g == 0:
            wait(load_out)
        updated(buf_in.at[b], hid, w_out, buf_out.at[b])
        start(departures(buf_out, out, row_of, sem_out, g, b))
        if g == 0:
            load_flux.wait()
        f = jnp.dot(w_flux[...], hid[...], preferred_element_type=jnp.float32)
        for j in range(GROUP):
            flux[g * GROUP + j] = f[:, j * cols : (j + 1) * cols]
    save = pltpu.make_async_copy(flux, flux_hbm, sem_f.at[1])
    save.start()
    for g in range(max(groups - 2, 0), groups):
        wait(departures(buf_out, out, row_of, sem_out, g, g % 2))
    save.wait()


def staying_kernel(
    devices, nnarrow,
    order, state, w_in_hbm, w_out_hbm, w_flux_hbm, flux_away_hbm, meta_hbm, owner_hbm, slot_hbm, weight_hbm,
    hidden, kept, w_out, keep, send,
    w_in, w_flux, flux_away, meta, owner, slot, weight, cells, areas, lows, flux, left, right, total,
    sem_w, sem_s, sem_kept,
):
    groups, _, _, cols = kept.shape
    stay = groups * GROUP
    move = flux_away.shape[0]
    blocks = stay + move
    device = lax.axis_index("wide") * nnarrow + lax.axis_index("narrow")

    def arrivals(g):
        return arrivals_of(state, lambda k: order[k], kept, sem_kept, g, g)

    load_in = row_parts(w_in_hbm, w_in, sem_w.at[0])
    load_out = row_parts(w_out_hbm, w_out, sem_w.at[1])
    pairs = [
        (w_flux_hbm, w_flux), (owner_hbm, owner), (slot_hbm, slot), (weight_hbm, weight),
        (flux_away_hbm, flux_away), (meta_hbm, meta),
    ]
    small = [pltpu.make_async_copy(src, dst, sem_s.at[i]) for i, (src, dst) in enumerate(pairs)]
    start(arrivals(0))
    start(load_in)
    start(small)

    def tables():
        for c in range(blocks):
            here = pl.ds(order[c], 1)
            if c < stay:
                cells[c : c + 1, :] = (owner[here, :] * OCN_DEV + slot[here, :]).astype(jnp.float32)
                areas[c : c + 1, :] = weight[here, :]
            else:
                dest = order[blocks + order[c]]
                cells[c : c + 1, :] = meta[dest, 0:1, :]
                areas[c : c + 1, :] = meta[dest, 1:2, :]
        high, low = spread(devices, device, cells[...].astype(jnp.int32))
        cells[...] = high.astype(jnp.float32)
        lows[...] = low.astype(jnp.float32).T

    def factors(c, at, f):
        if isinstance(c, int):
            row, low = slice(c, c + 1), lows[:, c : c + 1]
        else:
            row = pl.ds(c, 1)
            lane = lax.broadcasted_iota(jnp.int32, (cols, blocks), 1)
            low = jnp.sum(jnp.where(lane == c, lows[...], 0.0), axis=1, keepdims=True)
        fill(at, devices * OCN_DEV // LANES, f, areas[row, :], cells[row, :], low, left, right)

    def one_hot(g, j):
        factors(g * GROUP + j, j * cols, flux[j])

    def work(g, beside):
        hidden_of(side_by_side(kept.at[g]), w_in, hidden.at[g], beside)
        f = jnp.dot(w_flux[...], hidden[g], preferred_element_type=jnp.float32)
        for j in range(GROUP):
            flux[j] = f[:, j * cols : (j + 1) * cols]

    wait(arrivals(0))
    wait(load_in)
    if groups > 1:
        start(arrivals(1))
    wait(small)
    tables()
    work(0, lambda i: None)

    def later(g):
        wait(arrivals(g))
        work(g, lambda i: one_hot(g - 1, i) if i < GROUP else None)

    if devices <= 32:
        for g in range(1, groups):
            if g + 1 < groups:
                start(arrivals(g + 1))
            else:
                start(load_out)
            later(g)
            add_product(total, left, right, g == 1)
    else:
        total[...] = jnp.zeros_like(total)

        @pl.loop(1, groups)
        def _(g):
            @pl.when(g + 1 < groups)
            def _():
                start(arrivals(g + 1))

            @pl.when(g + 1 == groups)
            def _():
                start(load_out)

            later(g)
            add_product(total, left, right, False)

    for j in range(GROUP):
        one_hot(groups - 1, j)
    add_product(total, left, right, False)
    for g in range(move // GROUP):
        for j in range(GROUP):
            k = g * GROUP + j
            factors(stay + k, j * cols, flux_away[k])
        add_product(total, left, right, False)
    half = total.shape[0] // 2
    keep[...] = total[:half, :]
    send[...] = total[half:, :].astype(jnp.bfloat16)
    wait(load_out)


def update_kernel(first, last, order, kept, hidden, w_out, *rest):
    out, buf_out, sem_out = rest[-3:]

    def slot_of(k):
        return order[k]

    @pl.loop(first, last)
    def _(g):
        updated(kept.at[g], hidden.at[g], w_out, buf_out.at[g - first])
        start(departures(buf_out, out, slot_of, sem_out, g, g - first))

    for g in range(first, last):
        wait(departures(buf_out, out, slot_of, sem_out, g, g - first))


def spread(devices, device, cell):
    bits = devices.bit_length() - 1
    apart = (cell // OCN_DEV) ^ device
    far = jnp.zeros_like(apart)
    for i in range(bits):
        far = far | (((apart >> i) & 1) << (bits - 1 - i))
    return far * (OCN_DEV // LANES) + cell % OCN_DEV // LANES, cell % LANES


def fill(at, highs, f, area, high, low, left, right):
    nflux, cols = f.shape
    bf16 = jnp.bfloat16
    f = (f * area).astype(bf16)
    high = jnp.broadcast_to(high, (nflux, cols)).astype(bf16)
    low = jnp.broadcast_to(low, (cols, LANES)).astype(bf16)
    lanes = lax.broadcasted_iota(jnp.int32, (cols, LANES), 1).astype(jnp.float32).astype(bf16)
    one, zero = jnp.ones((), bf16), jnp.zeros((), bf16)
    right[at : at + cols, :] = jnp.where(low == lanes, one, zero)
    for h in range(highs):
        left[h * nflux : (h + 1) * nflux, at : at + cols] = jnp.where(
            high == jnp.asarray(h, bf16), f, zero
        )


def add_product(total, left, right, first):
    h = right[...]
    for r in range(0, total.shape[0], CHUNK):
        p = jnp.dot(left[r : r + CHUNK, :], h, preferred_element_type=jnp.float32)
        total[r : r + CHUNK, :] = p if first else total[r : r + CHUNK, :] + p


def halve_kernel(mine, came, keep, *sends):
    rows = keep.shape[0]
    keep[...] = mine[:rows, :] + came[:rows, :].astype(jnp.float32)
    for i, send in enumerate(sends):
        at = pl.ds((i + 1) * rows, rows)
        send[...] = (mine[at, :] + came[at, :].astype(jnp.float32)).astype(jnp.bfloat16)


def place_kernel(move, order, arrived, _, out, sem):
    blocks = out.shape[0]
    stay = blocks - move
    copies = []
    for k in range(move):
        s = order[stay + k]
        copies.append(
            pltpu.make_async_copy(arrived.at[order[2 * blocks + s]], out.at[s], sem.at[k])
        )
    start(copies)
    wait(copies)


def last_kernel(mine, *rest):
    came, ocean = rest[:-2], rest[-1]
    nflux = ocean.shape[0]
    for h in range(OCN_DEV // LANES):
        rows = slice(h * nflux, (h + 1) * nflux)
        part = mine[rows, :]
        for c in came:
            part = part + c[rows, :].astype(jnp.float32)
        ocean[:, h * LANES : (h + 1) * LANES] = part


SMEM = pl.BlockSpec(memory_space=pltpu.SMEM)
VMEM = pl.BlockSpec(memory_space=pltpu.VMEM)
HBM = pl.BlockSpec(memory_space=pltpu.HBM)
ANY = pl.BlockSpec(memory_space=pl.ANY)


def per_device(state, group_of, w_in, w_out, w_flux, owner, ocean_slot, remap_weight):
    nwide = lax.axis_size("wide")
    nnarrow = lax.axis_size("narrow")
    blocks, depth, cols = state.shape
    inner = w_in.shape[0]
    nflux = w_flux.shape[0]
    devices = nwide * nnarrow
    move = nwide // 2
    stay = blocks - move
    bf16, f32, i32 = jnp.bfloat16, jnp.float32, jnp.int32
    shape = jax.ShapeDtypeStruct
    dma = pltpu.SemaphoreType.DMA
    side = GROUP * cols
    owner = owner[:, 0].reshape(blocks, cols)
    slot = ocean_slot.reshape(blocks, cols)
    weight = remap_weight.reshape(blocks, cols)
    params = pltpu.CompilerParams(vmem_limit_bytes=20 * MIB)
    in_hbm = functools.partial(pltpu.with_memory_space_constraint, memory_space=pltpu.HBM)
    in_vmem = functools.partial(pltpu.with_memory_space_constraint, memory_space=pltpu.VMEM)

    def cost(n, products):
        return pl.CostEstimate(
            flops=2 * n * cols * inner * depth * products,
            bytes_accessed=4 * n * depth * cols + 2 * inner * depth * products,
            transcendentals=n * cols * inner,
        )

    def swap(x, axis, bit):
        return lax.ppermute(x, axis, [(i, i ^ bit) for i in range(lax.axis_size(axis))])

    with jax.named_scope("order_of_blocks"):
        order, meta = pl.pallas_call(
            functools.partial(order_kernel, nwide, nnarrow, move),
            out_shape=(pltpu.HBM((3 * blocks,), i32), pltpu.HBM((nwide, 8, cols), f32)),
            in_specs=[HBM] * 4,
            out_specs=(HBM, HBM),
            scratch_shapes=[
                pltpu.SMEM((3 * blocks,), i32),
                pltpu.SMEM(group_of.shape, i32),
                pltpu.VMEM((blocks, cols), i32),
                pltpu.VMEM((blocks, cols), i32),
                pltpu.VMEM((blocks, cols), f32),
                pltpu.VMEM((nwide, 8, cols), f32),
                dma((6,)),
            ],
            compiler_params=params,
        )(in_hbm(group_of), in_hbm(owner), in_hbm(slot), in_hbm(weight))
    meta = lax.all_to_all(meta, "wide", split_axis=0, concat_axis=0, tiled=True)

    groups = stay // GROUP
    parts = max(inner, depth) // STEP
    with jax.named_scope("leaving_blocks"):
        outgoing, flux_away = pl.pallas_call(
            leaving_kernel,
            out_shape=(pltpu.HBM((nwide, depth, cols), bf16), pltpu.HBM((move, nflux, cols), f32)),
            in_specs=[HBM] * 5,
            out_specs=(HBM, HBM),
            scratch_shapes=[
                pltpu.VMEM((inner, depth), bf16),
                pltpu.VMEM((depth, inner), bf16),
                pltpu.VMEM((nflux, inner), bf16),
                pltpu.VMEM((move, nflux, cols), f32),
                pltpu.SMEM((3 * blocks,), i32),
                pltpu.VMEM((2, GROUP, depth, cols), bf16),
                pltpu.VMEM((2, GROUP, depth, cols), bf16),
                pltpu.VMEM((inner, side), bf16),
                dma((2, parts)),
                dma((3,)),
                dma((2, GROUP)),
                dma((2, GROUP)),
            ],
            compiler_params=params,
            cost_estimate=cost(move, 2),
        )(in_hbm(order), in_hbm(state), in_hbm(w_in), in_hbm(w_out), in_hbm(w_flux))
    outgoing, meta = lax.optimization_barrier((outgoing, meta))
    arrived = lax.all_to_all(outgoing, "wide", split_axis=0, concat_axis=0, tiled=True)

    rows = devices * nflux * OCN_DEV // LANES
    with jax.named_scope("staying_blocks_and_cell_sums"):
        hidden, kept, w_out, keep, send = pl.pallas_call(
            functools.partial(staying_kernel, devices, nnarrow),
            out_shape=(
                pltpu.VMEM((groups, inner, side), bf16),
                pltpu.VMEM((groups, GROUP, depth, cols), bf16),
                pltpu.VMEM(w_out.shape, bf16),
                shape((rows // 2, LANES), f32),
                shape((rows // 2, LANES), bf16),
            ),
            in_specs=[SMEM] + [HBM] * 9,
            out_specs=(VMEM,) * 5,
            scratch_shapes=[
                pltpu.VMEM((inner, depth), bf16),
                pltpu.VMEM((nflux, inner), bf16),
                pltpu.VMEM((move, nflux, cols), f32),
                pltpu.VMEM((nwide, 8, cols), f32),
                pltpu.VMEM((blocks, cols), i32),
                pltpu.VMEM((blocks, cols), i32),
                pltpu.VMEM((blocks, cols), f32),
                pltpu.VMEM((blocks, cols), f32),
                pltpu.VMEM((blocks, cols), f32),
                pltpu.VMEM((cols, blocks), f32),
                pltpu.VMEM((GROUP, nflux, cols), f32),
                pltpu.VMEM((rows, side), bf16),
                pltpu.VMEM((side, LANES), bf16),
                pltpu.VMEM((rows, LANES), f32),
                dma((2, parts)),
                dma((6,)),
                dma((groups, GROUP)),
            ],
            compiler_params=pltpu.CompilerParams(vmem_limit_bytes=20 * MIB + 14 * rows * LANES),
            cost_estimate=pl.CostEstimate(
                flops=2 * cols * (stay * inner * depth + rows * LANES * blocks),
                bytes_accessed=2 * stay * depth * cols + 4 * inner * depth,
                transcendentals=stay * cols * inner,
            ),
        )(
            order,
            *map(in_hbm, (state, w_in, w_out, w_flux, flux_away, meta, owner, slot, weight)),
        )

    partial = None
    done = 0

    def update(upto, partial, after):
        begun = () if partial is None else (partial,)
        return pl.pallas_call(
            functools.partial(update_kernel, done, upto),
            out_shape=shape(state.shape, bf16),
            in_specs=[SMEM, VMEM, VMEM, VMEM, ANY] + [ANY] * len(begun),
            out_specs=ANY,
            scratch_shapes=[
                pltpu.VMEM((upto - done, GROUP, depth, cols), bf16),
                dma((upto - done, GROUP)),
            ],
            input_output_aliases={5: 0} if begun else {},
            compiler_params=params,
            cost_estimate=cost((upto - done) * GROUP, 1),
        )(order, in_vmem(kept), in_vmem(hidden), in_vmem(w_out), after, *begun)

    bits = [("narrow", 1 << i) for i in range(nnarrow.bit_length() - 1)]
    bits += [("wide", 1 << i) for i in range(nwide.bit_length() - 3)]
    own = nflux * OCN_DEV // LANES
    rows //= 2
    sends = (send,)
    with jax.named_scope("ocean_sums"):
        for i, (axis, bit) in enumerate(bits):
            came = swap(sends[0], axis, bit)
            if i > 0:
                upto = min(groups, done + -(-groups // len(bits)))
                if upto > done:
                    with jax.named_scope("update_of_staying_blocks"):
                        partial = update(upto, partial, keep)
                    done = upto
            quarters = i == len(bits) - 1
            rows = own if quarters else rows // 2
            count = 3 if quarters else 1
            keep, *sends = pl.pallas_call(
                halve_kernel,
                out_shape=(shape((rows, LANES), f32),) + (shape((rows, LANES), bf16),) * count,
                in_specs=[VMEM, VMEM],
                out_specs=(VMEM,) * (1 + count),
                compiler_params=params,
            )(keep, came)
        came = [swap(x, "wide", d * nwide // 4) for x, d in zip(sends, (2, 1, 3))]
        with jax.named_scope("update_of_staying_blocks"):
            partial = update(groups, partial, keep)

    with jax.named_scope("arrived_blocks"):
        new_state = pl.pallas_call(
            functools.partial(place_kernel, move),
            out_shape=shape(state.shape, bf16),
            in_specs=[SMEM, VMEM, ANY],
            out_specs=ANY,
            scratch_shapes=[dma((move,))],
            input_output_aliases={2: 0},
            compiler_params=params,
        )(order, arrived, partial)
    with jax.named_scope("last_sums"):
        ocean = pl.pallas_call(
            last_kernel,
            out_shape=shape((nflux, OCN_DEV), f32),
            in_specs=[VMEM] * 4 + [HBM],
            out_specs=VMEM,
            compiler_params=params,
        )(keep, *came, in_hbm(new_state))
    return (new_state, ocean)


def solution(mesh):
    in_specs = (
        P(("wide", "narrow"), None, None),
        P(),
        P(),
        P(),
        P(),
        P(("wide", "narrow"), None),
        P(("wide", "narrow")),
        P(("wide", "narrow")),
    )
    out_specs = (P(("wide", "narrow"), None, None), P(None, ("wide", "narrow")))
    return jax.shard_map(
        per_device, mesh=mesh, in_specs=in_specs, out_specs=out_specs, check_vma=False
    )
```
